512 devices in a mesh: row: 16 (over y, z_hi), col: 32 (over z_lo, x, core).
Axes of the slice: x: 4, y: 8, z: 8 (z_hi: 2, z_lo: 4; z = z_hi * 4 + z_lo), core: 2. Of those that a mesh axis runs over, the one named last changes fastest.
Arguments:
- question_vectors: float32 [2048, 4096], P('row', 'col'), may hold values from -1 to 1
- document_vectors: float32 [8192, 4096], P('col', 'row'), may hold values from -1 to 1
- positive: int32 [2048], P('row'), may hold values from 0 to 3
Outputs:
- loss_value: float32 [], replicated
- question_vector_derivative: float32 [2048, 4096], P('row', 'col')
- document_vector_derivative: float32 [8192, 4096], P('col', 'row')
The draws below stay inside these ranges and needn't reach their ends.
All inputs are finite; a program needn't handle non-finite values.
Results may differ from the reference program's by a relative error of at most 0.00065.
Values sent between devices are 32-bit elements; how exact they have to be, the bound alone decides.
A program may use at most 64 MiB of HBM per device.

```python
import math
import jax
import jax.numpy as jnp
from jax import lax

D = 4096
LIST = 4
NQ = 2048
NP = 8192


def drawn_rows(key, lower_level, upper_level):
    sign_key, level_key, pick_key = jax.random.split(key, 3)
    sign_values = jax.random.rademacher(sign_key, (NQ, D), jnp.float32)
    magnitude = lower_level + (upper_level - lower_level) * jax.random.uniform(level_key, (NQ, 1), jnp.float32)
    chosen = jax.random.randint(pick_key, (NQ, 1), 0, 8) == 0
    return (sign_values * (magnitude / math.sqrt(D)), magnitude, chosen)


def row_scales(scale_key, row_total, lower_end, upper_end):
    uniform_part = jax.random.uniform(scale_key, (row_total, 1), jnp.float32)
    return jnp.exp(math.log(lower_end) + uniform_part * (math.log(upper_end) - math.log(lower_end)))


def listed_rows(listed_key, aligned, magnitude, chosen, scatter_noise, lower_copy):
    copy_key, gap_key, jitter_key = jax.random.split(listed_key, 3)
    copy_level = lower_copy + (1.0 - lower_copy) * jax.random.uniform(copy_key, (NQ, 1), jnp.float32)
    score_gap = 1.0 + 2.0 * jax.random.uniform(gap_key, (NQ, 1), jnp.float32)
    jitter = 0.003 * jnp.clip(jax.random.normal(jitter_key, (NQ, D), jnp.float32), -5.0, 5.0)
    first_copy = copy_level * aligned
    second_copy = (copy_level - score_gap * 0.05 / (magnitude * magnitude)) * aligned + jitter
    first_rows = jnp.repeat(first_copy, LIST, axis=0)
    second_rows = jnp.repeat(second_copy, LIST, axis=0)
    lifted = jnp.repeat(chosen, LIST, axis=0)
    slot_index = jnp.arange(NP, dtype=jnp.int32) % LIST
    first_slot = (slot_index == 0)[:, None]
    second_slot = (slot_index == 1)[:, None]
    picked = jnp.where(lifted & first_slot, first_rows, jnp.where(lifted & second_slot, second_rows, scatter_noise))
    return jnp.clip(picked, -1.0, 1.0)


def draw_question_vectors(key, part):
    aligned, magnitude, chosen = drawn_rows(key, 4.0, 6.0)
    key = jax.random.fold_in(key, 11)
    noise_key, scale_key = jax.random.split(key)
    scatter_noise = 0.04 * jnp.clip(jax.random.normal(noise_key, (NQ, D), jnp.float32), -5.0, 5.0)
    scatter_noise = scatter_noise * row_scales(scale_key, NQ, 0.5, 2.0)
    return jnp.clip(jnp.where(chosen, aligned, scatter_noise), -1.0, 1.0)


def draw_document_vectors(key, part):
    aligned, magnitude, chosen = drawn_rows(key, 4.0, 6.0)
    key = jax.random.fold_in(key, 23)
    noise_key, scale_key, listed_key = jax.random.split(key, 3)
    scatter_noise = 0.04 * jnp.clip(jax.random.normal(noise_key, (NP, D), jnp.float32), -5.0, 5.0)
    scatter_noise = scatter_noise * row_scales(scale_key, NP, 0.5, 2.0)
    return listed_rows(listed_key, aligned, magnitude, chosen, scatter_noise, 0.5)


def place_ends(drawn, key, least, largest):
    place = [jax.random.randint(jax.random.fold_in(key, axis), (), 0, length) for axis, length in enumerate(drawn.shape)]
    main_axis = drawn.shape.index(max(drawn.shape))
    beside = place[:main_axis] + [(place[main_axis] + 1) % drawn.shape[main_axis]] + place[main_axis + 1:]
    return drawn.at[tuple(place)].set(least).at[tuple(beside)].set(largest)


def setup_inputs(seed: int = 0) -> dict:
    splits = jax.random.split(jax.random.key(seed), 4)
    return {
        "question_vectors": draw_question_vectors(jax.random.fold_in(splits[3], 71), 0),
        "document_vectors": draw_document_vectors(jax.random.fold_in(splits[3], 71), 0),
        "positive": place_ends(jax.random.randint(splits[2], (NQ,), 0, LIST), jax.random.fold_in(splits[2], 1), 0, LIST - 1).astype(jnp.int32),
    }


sharpness_divisor = 0.05


def reference(question_vectors, document_vectors, positive):
    biggest_match_level = lax.Precision.HIGHEST
    match_raw_levels = jnp.dot(question_vectors, document_vectors.T, precision=biggest_match_level, preferred_element_type=jnp.float32) / sharpness_divisor
    topmost = jnp.max(match_raw_levels, axis=1)
    exp_total = jnp.sum(jnp.exp(match_raw_levels - topmost[:, None]), axis=1)
    log_total = topmost + jnp.log(exp_total)
    target_index = LIST * jnp.arange(NQ, dtype=jnp.int32) + positive.astype(jnp.int32)
    passage_index = jnp.arange(NP, dtype=jnp.int32)
    positive_hit = (target_index[:, None] == passage_index[None, :]).astype(jnp.float32)
    positive_score = jnp.sum(match_raw_levels * positive_hit, axis=1)
    loss_value = jnp.mean(log_total - positive_score)
    normalized_likelihoods = jnp.exp(match_raw_levels - log_total[:, None]) - positive_hit
    question_vector_derivative = jnp.dot(normalized_likelihoods, document_vectors, precision=biggest_match_level, preferred_element_type=jnp.float32) / sharpness_divisor
    document_vector_derivative = jnp.dot(normalized_likelihoods.T, question_vectors, precision=biggest_match_level, preferred_element_type=jnp.float32) / sharpness_divisor
    return loss_value, question_vector_derivative, document_vector_derivative
```

```python
import jax
import jax.numpy as jnp
from jax import lax
from jax.experimental import pallas as pl
from jax.experimental.pallas import tpu as pltpu
from jax.sharding import PartitionSpec as P

LIST = 4
NQ = 2048
INV = 20.0

K = 4
R = 64 // K
DP = 2
N_SEM = 47 * K + 24
ORDER = (
    1, 3, 4, 5, 6, 7, 8, 11, 12, 13, 15, 16, 17, 18, 19, 22, 23, 24, 26, 27, 28, 29, 30, 33, 34, 35, 37, 38,
    39, 40, 41, 44, 45, 46, 14, 25, 36, 0, 9, 20, 31, 42, 2, 10, 21, 32, 43, 0, 0, 3, 0, 0, 0, 14, 25, 36, 3,
    0, 14, 3, 3, 25, 0, 36, 14, 14, 3, 25, 25, 3, 36, 36, 14, 14, 4, 5, 25, 25, 36, 36, 15, 4, 16, 5, 26, 27,
    15, 4, 16, 37, 38, 26, 27, 15, 6, 37, 38, 26, 17, 37, 8, 7, 6, 28, 18, 19, 8, 7, 39, 17, 29, 30, 6, 18,
    19, 7, 28, 40, 41, 29, 39, 30, 17, 18, 40, 28, 41, 29, 39, 40, 9, 20, 10, 31, 11, 12, 42, 22, 23, 21, 32,
    13, 33, 34, 42, 24, 43, 2, 35, 1, 44, 45, 13, 2, 46, 24, 1, 1, 1, 1, 35, 13, 24, 46, 2, 1, 35, 46,
)

MESH = pl.DeviceIdType.MESH
F32 = jnp.float32
BF16 = jnp.bfloat16


def split2(a):
    hi = a.astype(BF16)
    return hi, (a - hi.astype(F32)).astype(BF16)


def split3(a):
    p1 = a.astype(BF16)
    r1 = a - p1.astype(F32)
    p2 = r1.astype(BF16)
    return p1, p2, (r1 - p2.astype(F32)).astype(BF16)


def dot_nt(a, b):
    return lax.dot_general(a, b, (((1,), (1,)), ((), ())), preferred_element_type=F32)


def dot_nn(a, b):
    return lax.dot_general(a, b, (((1,), (0,)), ((), ())), preferred_element_type=F32)


def dot_tn(a, b):
    return lax.dot_general(a, b, (((0,), (0,)), ((), ())), preferred_element_type=F32)


def kernel(
    q_ref, d_ref, pos_hbm, loss_ref, dq_ref, dd_ref,
    qbuf, qs, dbuf, ds_, dra, drb, sbuf, rl, rs, sg, ws, tcol, pack, tpack,
    stx, stz, tg, dqp, dqa, dqb, dxl, dxr, dz, dqt, dqo,
    dd, ddr, ddt, era, erb, ddz, lsum, lrecv, pos_ref, ssem, rsem, lsem,
):
    row = lax.axis_index("row")
    col = lax.axis_index("col")
    y, zh = lax.div(row, 2), lax.rem(row, 2)
    zl, core = lax.div(col, 8), lax.rem(col, 2)
    x = lax.rem(lax.div(col, 2), 4)
    z = zh * 4 + zl

    def dev(xx, yy, zz, cc):
        return (yy * 2 + lax.div(zz, 4), (lax.rem(zz, 4) * 4 + xx) * 2 + cc)

    def at_y(d):
        return dev(x, lax.rem(y + d + 8, 8), z, core)

    def at_z(d):
        return dev(x, y, lax.rem(z + d + 8, 8), core)

    def at_zl(d):
        return dev(x, y, zh * 4 + lax.rem(zl + d, 4), core)

    def at_x(d):
        return dev(lax.rem(x + d + 4, 4), y, z, core)

    def xi(xx):
        return (1 - lax.rem(xx, 2)) * 2 + lax.div(xx, 2)

    def xo(d):
        return xi(lax.rem(x + d + 4, 4))

    def blk(d):
        yy = lax.rem(y + d + 8, 8)
        b = lax.rem(yy, 2) * 4 + lax.div(yy, 2)
        return pl.ds(pl.multiple_of(b * R, R), R)

    def blk_b(d):
        yy = lax.rem(y + d + 8, 8)
        return lax.rem(yy, 2) * 4 + lax.div(yy, 2)

    other = dev(x, y, z, 1 - core)
    hx = 2 * lax.rem(y, 2) + 1 - lax.rem(x, 2)
    hy = 2 * zl + lax.div(x, 2)
    hz = zh * 4 + lax.div(y, 2)
    home = [dev(hx, hy, hz, core), dev(hx, hy, hz, 1 - core)]

    barrier = pltpu.get_barrier_semaphore()
    partners = [other, at_z(2), at_z(-2), at_z(4)] + [at_y(t) for t in range(1, 8)]
    partners += [at_zl(t) for t in (1, 2, 3)] + [at_x(t) for t in (1, 2, 3)] + home
    for p in partners:
        pl.semaphore_signal(barrier, inc=1, device_id=p, device_id_type=MESH)

    own_p = pl.ds(pl.multiple_of(core * 256, 256), 256)
    oth_p = pl.ds(pl.multiple_of((1 - core) * 256, 256), 256)
    get_pos = pltpu.make_async_copy(pos_hbm, pos_ref, lsem.at[0])
    get_pos.start()
    get_d = pltpu.make_async_copy(d_ref, dbuf.at[zh, own_p], lsem.at[1])
    get_d.start()
    pack[...] = jnp.zeros_like(pack)
    tpack[...] = jnp.zeros_like(tpack)
    pidx = (512 * (zl * 4 + x) + lax.broadcasted_iota(jnp.int32, (1, 512), 1)).astype(F32)
    lane = lax.broadcasted_iota(jnp.int32, (1, 128), 1)
    get_pos.wait()
    target = (LIST * (row * 128 + lane) + pos_ref[...]).astype(F32)
    tcol[...] = jnp.broadcast_to(target, (128, 128)).T
    get_d.wait()
    pl.semaphore_wait(barrier, len(partners))

    sends = []

    def send(src, dst, to):
        i = len(sends)
        cp = pltpu.make_async_remote_copy(
            src_ref=src, dst_ref=dst, send_sem=ssem.at[i], recv_sem=rsem.at[i],
            device_id=to, device_id_type=MESH,
        )
        cp.start()
        sends.append(cp)
        return cp

    def rows(start, size):
        return pl.ds(pl.multiple_of(start, size), size)

    half = 128 // DP

    def z_exchange(src, mid_a, mid_b, dst_a, dst_b, base):
        a = [send(src.at[i * half : (i + 1) * half], mid_a.at[i * half : (i + 1) * half], at_z(2)) for i in range(DP)]
        b = [send(src.at[128 + i * half : 128 + (i + 1) * half], mid_b.at[i * half : (i + 1) * half], at_z(-2))
             for i in range(DP)]
        last = []
        for i in range(DP):
            rw = slice(i * half, (i + 1) * half)
            yield
            a[i].wait_recv()
            last.append(send(mid_a.at[rw], dst_a.at[rows(base + i * half, half)], at_z(2)))
            yield
            b[i].wait_recv()
            last.append(send(mid_b.at[rw], dst_b.at[rows(base + 128 + i * half, half)], at_z(-2)))
        return last

    def documents():
        c = send(d_ref, dbuf.at[zh, own_p], other)
        below = dbuf.at[lax.div(lax.rem(z + 6, 8), 4)]
        above = dbuf.at[lax.div(lax.rem(z + 2, 8), 4)]
        last = yield from z_exchange(d_ref, dra, drb, below, above, core * 256)
        yield
        c.wait_recv()
        yield
        for cp in last:
            cp.wait_recv()
        e = send(dbuf.at[1 - zh, own_p], dbuf.at[1 - zh, own_p], other)
        yield
        e.wait_recv()
        for fh in range(2):
            for i, part in enumerate(split3(dbuf[fh])):
                ds_[i, fh] = part

    state = {}

    class Chunk:
        def __init__(self, k):
            self.k = k
            self.far = 1 if k % 2 == 0 else -1
            self.to_far, self.to_near = at_y(self.far), at_y(-self.far)
            self.pr, self.pq = k // 2, (k % 2) * 8 * R

        def queries(self):
            k = self.k
            cps = []
            for j in range(2):
                kc = core if j == 0 else 1 - core
                cps.append(send(
                    q_ref.at[rows(64 * kc + R * k, R)],
                    qbuf.at[k, lax.rem(x, 2) * 2 + lax.rem(y, 2), rows(lax.div(y, 2) * R, R),
                            pl.ds(pl.multiple_of(core * 128, 128), 128)],
                    home[j],
                ))
            yield
            for cp in cps:
                cp.wait_recv()
            mine = qbuf.at[k, xo(0), rows(zl * R, R)]
            cps = [send(mine, mine, at_zl(t)) for t in (1, 2, 3)]
            yield
            for cp in cps:
                cp.wait_recv()
            mine = qbuf.at[k, xo(0)]
            cr = send(mine, mine, at_x(1))
            cl = send(mine, mine, at_x(-1))
            yield
            cr.wait_recv()
            part = qbuf.at[k, xo(-1), 0 : 2 * R]
            rr = send(part, part, at_x(1))
            yield
            cl.wait_recv()
            part = qbuf.at[k, xo(1), 2 * R : 4 * R]
            rel = send(part, part, at_x(-1))
            yield
            rr.wait_recv()
            rel.wait_recv()
            for fh in range(2):
                whole = qbuf[k, 2 * fh : 2 * fh + 2].reshape(8 * R, 256)
                for i, part in enumerate(split3(whole)):
                    qs[self.pr, i, fh, self.pq : self.pq + 8 * R, :] = part
            yield

            def scores(i, carry):
                rw = pl.ds(pl.multiple_of(i * 128, 128), 128)
                qw = pl.ds(pl.multiple_of(self.pq + i * 128, 128), 128)
                acc = None
                for a, b in ((2, 0), (1, 1), (0, 2), (1, 0), (0, 1), (0, 0)):
                    for fh in range(2):
                        t = dot_nt(qs[self.pr, a, fh, qw, :], ds_[b, fh])
                        acc = t if acc is None else acc + t
                sbuf[k, rw, :] = acc
                return carry

            lax.fori_loop(0, 8 * R // 128, scores, 0)
            self.cf = send(sbuf.at[k, blk(4 * self.far)], rl.at[k, 0], self.to_far)
            self.cn = send(sbuf.at[k, blk(-3 * self.far)], rs.at[k, 0], self.to_near)

        def reduce_far(self):
            k = self.k
            for s in range(3):
                yield
                self.cf.wait_recv()
                rl[k, s] = rl[k, s] + sbuf[k, blk(self.far * (3 - s)), :]
                self.cf = send(rl.at[k, s], rl.at[k, s + 1], self.to_far)

        def reduce_near(self):
            k = self.k
            for s in range(2):
                yield
                self.cn.wait_recv()
                rs[k, s] = rs[k, s] + sbuf[k, blk(-self.far * (2 - s)), :]
                self.cn = send(rs.at[k, s], rs.at[k, s + 1], self.to_near)

        def join(self):
            k = self.k
            yield
            self.cf.wait_recv()
            self.cn.wait_recv()
            full = (sbuf[k, blk(0), :] + rs[k, 2] + rl[k, 3]) * INV
            sg[k, blk(0), :] = full
            mine = sg.at[k, blk(0)]
            self.af = send(mine, mine, self.to_far)
            self.an = send(mine, mine, self.to_near)
            tc = tcol[rows(64 * core + R * k, R), 0:1]
            top = jnp.max(full, axis=1, keepdims=True)
            total = jnp.sum(jnp.exp(full - top), axis=1, keepdims=True)
            hit = jnp.sum(jnp.where(tc == pidx, full, 0.0), axis=1, keepdims=True)
            ln = lax.broadcasted_iota(jnp.int32, (R, 128), 1)
            pack[k, 0:R, :] = jnp.where(ln == 0, top, jnp.where(ln == 1, total, jnp.where(ln == 2, hit, tc)))
            stx[k, x] = pack[k].T[0:8]
            cps = [send(stx.at[k, x], stx.at[k, x], at_x(t)) for t in (1, 2, 3)]
            yield
            for cp in cps:
                cp.wait_recv()
            stz[k, zl] = tile(*merge(stx[k]))
            cps = [send(stz.at[k, zl], stz.at[k, zl], at_zl(t)) for t in (1, 2, 3)]
            yield
            for cp in cps:
                cp.wait_recv()
            top, total, hit, tgt = merge(stz[k])
            mine = tg.at[k, blk_b(0)]
            tg[k, blk_b(0)] = tile(top + jnp.log(total), hit, tgt, tgt)
            self.g = [send(mine, mine, at_y(t)) for t in range(1, 8)]

        def gather_far(self):
            for s in range(3):
                yield
                self.af.wait_recv()
                part = sg.at[self.k, blk(-self.far * (1 + s))]
                self.af = send(part, part, self.to_far)

        def gather_near(self):
            for s in range(2):
                yield
                self.an.wait_recv()
                part = sg.at[self.k, blk(self.far * (1 + s))]
                self.an = send(part, part, self.to_near)

        def weights(self):
            k, pr, pq = self.k, self.pr, self.pq
            yield
            self.af.wait_recv()
            self.an.wait_recv()
            for cp in self.g:
                cp.wait_recv()
            for b in range(8):
                tpack[k, b : b + 1, :] = tg[k, b, 0:1, :]
                tpack[k, 8 + b : 9 + b, :] = tg[k, b, 2:3, :]
            tt = tpack[k].T
            for b in range(8):
                w = jnp.exp(sg[k, b * R : (b + 1) * R, :] - tt[0:R, b : b + 1])
                w = (w - jnp.where(tt[0:R, 8 + b : 9 + b] == pidx, 1.0, 0.0)) * INV
                w1, w2 = split2(w)
                ws[pr, 0, pq + b * R : pq + (b + 1) * R, :] = w1
                ws[pr, 1, pq + b * R : pq + (b + 1) * R, :] = w2
            if k == K - 1:
                yield
                self.dd_pair(1 - zh)
                state["e0"] = send(dd.at[1 - zh, oth_p], ddr.at[0], other)

            def some(i, carry):
                rw = pl.ds(pl.multiple_of(pq + i * 4 * R, 4 * R), 4 * R)
                for fh in range(2):
                    acc = dot_nn(ws[pr, 1, rw, :], ds_[0, fh])
                    acc = acc + dot_nn(ws[pr, 0, rw, :], ds_[1, fh])
                    dqp[k, 2 * fh + i] = acc + dot_nn(ws[pr, 0, rw, :], ds_[0, fh])
                return carry

            lax.fori_loop(0, 2, some, 0)
            self.ca = send(dqp.at[k, xo(2), 0 : 2 * R], dqa.at[k], at_x(1))
            self.cb = send(dqp.at[k, xo(2), 2 * R : 4 * R], dqb.at[k], at_x(-1))
            self.c1 = send(dqp.at[k, xo(1), 2 * R : 4 * R], dxl.at[k, 2 * R : 4 * R], at_x(1))
            self.c2 = send(dqp.at[k, xo(-1), 0 : 2 * R], dxr.at[k, 0 : 2 * R], at_x(-1))

        def dd_pair(self, fh):
            pr = self.pr
            acc = dot_tn(ws[pr, 1], qs[pr, 0, fh])
            acc = acc + dot_tn(ws[pr, 0], qs[pr, 1, fh])
            acc = acc + dot_tn(ws[pr, 0], qs[pr, 0, fh])
            if pr == 0:
                dd[fh] = acc
            else:
                dd[fh] = dd[fh] + acc

        def documents_term(self):
            yield
            if self.k == K - 1:
                self.dd_pair(zh)
                state["e1"] = send(dd.at[zh, oth_p], ddr.at[1], other)
            elif self.k % 2 == 1:
                self.dd_pair(0)
                self.dd_pair(1)

        def sum_right(self):
            k = self.k
            yield
            self.ca.wait_recv()
            dqa[k] = dqa[k] + dqp[k, xo(1), 0 : 2 * R, :]
            self.c3 = send(dqa.at[k], dxl.at[k, 0 : 2 * R], at_x(1))

        def sum_left(self):
            k = self.k
            yield
            self.cb.wait_recv()
            dqb[k] = dqb[k] + dqp[k, xo(-1), 2 * R : 4 * R, :]
            self.c4 = send(dqb.at[k], dxr.at[k, 2 * R : 4 * R], at_x(-1))

        def sum_join(self):
            k = self.k
            yield
            for cp in (self.c1, self.c2, self.c3, self.c4):
                cp.wait_recv()
            dqt[k] = dqp[k, xo(0)] + dxl[k] + dxr[k]
            cps = [send(dqt.at[k, rows(lax.rem(zl + t, 4) * R, R)], dz.at[k, t - 1], at_zl(t)) for t in (1, 2, 3)]
            yield
            for cp in cps:
                cp.wait_recv()
            mine = rows(zl * R, R)
            dqt[k, mine, :] = dqt[k, mine, :] + dz[k, 0] + dz[k, 1] + dz[k, 2]
            cps = []
            for j in range(2):
                kc = core if j == 0 else 1 - core
                cps.append(send(
                    dqt.at[k, mine, pl.ds(pl.multiple_of(kc * 128, 128), 128)],
                    dqo.at[rows(64 * core + R * k, R)],
                    home[j],
                ))
            yield
            for cp in cps:
                cp.wait_recv()

    sub = lax.broadcasted_iota(jnp.int32, (8, 128), 0)

    def merge(st):
        m = st[:, 0, :]
        top = jnp.max(m, axis=0, keepdims=True)
        total = jnp.sum(st[:, 1, :] * jnp.exp(m - top), axis=0, keepdims=True)
        hit = jnp.sum(st[:, 2, :], axis=0, keepdims=True)
        return top, total, hit, st[0, 3:4, :]

    def tile(a, b, c, d):
        return jnp.where(sub == 0, a, jnp.where(sub == 1, b, jnp.where(sub == 2, c, d)))

    def ending():
        yield
        state["e0"].wait_recv()
        ddt[...] = dd[1 - zh, own_p, :] + ddr[0]
        last = yield from z_exchange(ddt, era, erb, ddz, ddz, 0)
        yield
        state["e1"].wait_recv()
        for cp in last:
            cp.wait_recv()
        dd_ref[...] = dd[zh, own_p, :] + ddr[1] + ddz[...]

    def loss():
        yield
        part = jnp.zeros((8, 128), F32)
        for k in range(K):
            part = part + jnp.where(lane < R, tg[k, :, 0, :] - tg[k, :, 1, :], 0.0)
        lsum[0] = jnp.broadcast_to(jnp.sum(part, keepdims=True), (8, 128))
        cp = send(lsum.at[0], lrecv.at[0], other)
        yield
        cp.wait_recv()
        lsum[1] = lsum[0] + lrecv[0]
        cp = send(lsum.at[1], lrecv.at[1], at_z(4))
        yield
        cp.wait_recv()
        loss_ref[0, 0] = jnp.sum((lsum[1] + lrecv[1])[0:1, 0:1]) * (1.0 / NQ)

    threads = [documents(), ending(), loss()]
    for k in range(K):
        c = Chunk(k)
        threads += [
            c.queries(), c.reduce_far(), c.reduce_near(), c.join(), c.gather_far(), c.gather_near(),
            c.weights(), c.documents_term(), c.sum_right(), c.sum_left(), c.sum_join(),
        ]
    ended = 0
    for t in ORDER:
        if next(threads[t], True):
            ended += 1
    assert ended == len(threads)
    dq_ref[...] = dqo[...]
    for cp in sends:
        cp.wait_send()


def fused(question_vectors, document_vectors, positive):
    vmem = pl.BlockSpec(memory_space=pltpu.VMEM)
    hbm = pl.BlockSpec(memory_space=pl.ANY)
    smem = pl.BlockSpec(memory_space=pltpu.SMEM)
    v = pltpu.VMEM
    loss, dq, dd = pl.pallas_call(
        kernel,
        out_shape=(
            jax.ShapeDtypeStruct((1, 1), F32),
            jax.ShapeDtypeStruct((128, 128), F32),
            jax.ShapeDtypeStruct((256, 256), F32),
        ),
        in_specs=[hbm, hbm, hbm],
        out_specs=(smem, vmem, vmem),
        scratch_shapes=[
            v((K, 4, 4 * R, 256), F32),
            v((K // 2, 3, 2, 16 * R, 256), BF16),
            v((2, 512, 256), F32),
            v((3, 2, 512, 256), BF16),
            v((128, 256), F32),
            v((128, 256), F32),
            v((K, 8 * R, 512), F32),
            v((K, 4, R, 512), F32),
            v((K, 3, R, 512), F32),
            v((K, 8 * R, 512), F32),
            v((K // 2, 2, 16 * R, 512), BF16),
            v((128, 128), F32),
            v((K, 128, 128), F32),
            v((K, 128, 128), F32),
            v((K, 4, 8, 128), F32),
            v((K, 4, 8, 128), F32),
            v((K, 8, 8, 128), F32),
            v((K, 4, 4 * R, 256), F32),
            v((K, 2 * R, 256), F32),
            v((K, 2 * R, 256), F32),
            v((K, 4 * R, 256), F32),
            v((K, 4 * R, 256), F32),
            v((K, 3, R, 256), F32),
            v((K, 4 * R, 256), F32),
            v((128, 128), F32),
            v((2, 512, 256), F32),
            v((2, 256, 256), F32),
            v((256, 256), F32),
            v((128, 256), F32),
            v((128, 256), F32),
            v((256, 256), F32),
            v((2, 8, 128), F32),
            v((2, 8, 128), F32),
            v((1, 128), jnp.int32),
            pltpu.SemaphoreType.DMA((N_SEM,)),
            pltpu.SemaphoreType.DMA((N_SEM,)),
            pltpu.SemaphoreType.DMA((2,)),
        ],
        compiler_params=pltpu.CompilerParams(
            collective_id=0, has_side_effects=True, vmem_limit_bytes=40 * 1024 * 1024
        ),
        name="infonce",
    )(question_vectors, document_vectors, positive.reshape(1, 128))
    return loss.reshape(()), dq, dd


def solution(mesh):
    in_specs = (P("row", "col"), P("col", "row"), P("row"))
    out_specs = (P(), P("row", "col"), P("col", "row"))
    return jax.shard_map(fused, mesh=mesh, in_specs=in_specs, out_specs=out_specs, check_vma=False)
```

```python
import jax
import jax.numpy as jnp
from jax import lax
from jax.experimental import pallas as pl
from jax.experimental.pallas import tpu as pltpu
from jax.sharding import PartitionSpec as P

LIST = 4
NQ = 2048
INV = 20.0

K = 4
R = 64 // K
DP = 2
N_SEM = 47 * K + 24
ORDER = (
    1, 3, 4, 5, 6, 7, 8, 11, 12, 13, 15, 16, 17, 18, 19, 22, 23, 24, 26, 27, 28, 29, 30, 33, 34, 35, 37, 38,
    39, 40, 41, 44, 45, 46, 14, 25, 36, 0, 9, 20, 31, 42, 2, 10, 21, 32, 43, 0, 0, 3, 0, 0, 0, 14, 25, 36, 3,
    0, 14, 3, 3, 25, 0, 36, 14, 14, 3, 25, 25, 3, 36, 36, 14, 14, 4, 5, 25, 25, 36, 36, 15, 4, 16, 5, 26, 27,
    15, 4, 16, 37, 38, 26, 27, 15, 6, 37, 38, 26, 17, 37, 8, 7, 6, 28, 18, 19, 8, 7, 39, 17, 29, 30, 6, 18,
    19, 7, 28, 40, 41, 29, 39, 30, 17, 18, 40, 28, 41, 29, 39, 40, 9, 20, 10, 31, 11, 12, 42, 22, 23, 21, 32,
    13, 33, 34, 42, 24, 43, 2, 35, 1, 44, 45, 13, 2, 46, 24, 1, 1, 1, 1, 35, 13, 24, 46, 2, 1, 35, 46,
)

MESH = pl.DeviceIdType.MESH
F32 = jnp.float32
BF16 = jnp.bfloat16


def split2(a):
    hi = a.astype(BF16)
    return hi, (a - hi.astype(F32)).astype(BF16)


def split3(a):
    p1 = a.astype(BF16)
    r1 = a - p1.astype(F32)
    p2 = r1.astype(BF16)
    return p1, p2, (r1 - p2.astype(F32)).astype(BF16)


def dot_nt(a, b):
    return lax.dot_general(a, b, (((1,), (1,)), ((), ())), preferred_element_type=F32)


def dot_nn(a, b):
    return lax.dot_general(a, b, (((1,), (0,)), ((), ())), preferred_element_type=F32)


def dot_tn(a, b):
    return lax.dot_general(a, b, (((0,), (0,)), ((), ())), preferred_element_type=F32)


def kernel(
    q_ref, d_ref, pos_hbm, loss_ref, dq_ref, dd_ref,
    qbuf, qs, dbuf, ds_, dra, drb, sbuf, rl, rs, sg, ws, tcol, pack, tpack,
    stx, stz, tg, dqp, dqa, dqb, dxl, dxr, dz, dqt, dqo,
    dd, ddr, ddt, era, erb, ddz, lsum, lrecv, pos_ref, ssem, rsem, lsem,
):
    row = lax.axis_index("row")
    col = lax.axis_index("col")
    y, zh = lax.div(row, 2), lax.rem(row, 2)
    zl, core = lax.div(col, 8), lax.rem(col, 2)
    x = lax.rem(lax.div(col, 2), 4)
    z = zh * 4 + zl

    def dev(xx, yy, zz, cc):
        return (yy * 2 + lax.div(zz, 4), (lax.rem(zz, 4) * 4 + xx) * 2 + cc)

    def at_y(d):
        return dev(x, lax.rem(y + d + 8, 8), z, core)

    def at_z(d):
        return dev(x, y, lax.rem(z + d + 8, 8), core)

    def at_zl(d):
        return dev(x, y, zh * 4 + lax.rem(zl + d, 4), core)

    def at_x(d):
        return dev(lax.rem(x + d + 4, 4), y, z, core)

    def xi(xx):
        return (1 - lax.rem(xx, 2)) * 2 + lax.div(xx, 2)

    def xo(d):
        return xi(lax.rem(x + d + 4, 4))

    def blk(d):
        yy = lax.rem(y + d + 8, 8)
        b = lax.rem(yy, 2) * 4 + lax.div(yy, 2)
        return pl.ds(pl.multiple_of(b * R, R), R)

    def blk_b(d):
        yy = lax.rem(y + d + 8, 8)
        return lax.rem(yy, 2) * 4 + lax.div(yy, 2)

    other = dev(x, y, z, 1 - core)
    hx = 2 * lax.rem(y, 2) + 1 - lax.rem(x, 2)
    hy = 2 * zl + lax.div(x, 2)
    hz = zh * 4 + lax.div(y, 2)
    home = [dev(hx, hy, hz, core), dev(hx, hy, hz, 1 - core)]

    barrier = pltpu.get_barrier_semaphore()
    partners = [other, at_z(2), at_z(-2), at_z(4)] + [at_y(t) for t in range(1, 8)]
    partners += [at_zl(t) for t in (1, 2, 3)] + [at_x(t) for t in (1, 2, 3)] + home
    for p in partners:
        pl.semaphore_signal(barrier, inc=1, device_id=p, device_id_type=MESH)

    own_p = pl.ds(pl.multiple_of(core * 256, 256), 256)
    oth_p = pl.ds(pl.multiple_of((1 - core) * 256, 256), 256)
    get_pos = pltpu.make_async_copy(pos_hbm, pos_ref, lsem.at[0])
    get_pos.start()
    get_d = pltpu.make_async_copy(d_ref, dbuf.at[zh, own_p], lsem.at[1])
    get_d.start()
    pack[...] = jnp.zeros_like(pack)
    tpack[...] = jnp.zeros_like(tpack)
    pidx = (512 * (zl * 4 + x) + lax.broadcasted_iota(jnp.int32, (1, 512), 1)).astype(F32)
    lane = lax.broadcasted_iota(jnp.int32, (1, 128), 1)
    get_pos.wait()
    target = (LIST * (row * 128 + lane) + pos_ref[...]).astype(F32)
    tcol[...] = jnp.broadcast_to(target, (128, 128)).T
    get_d.wait()
    pl.semaphore_wait(barrier, len(partners))

    sends = []

    def send(src, dst, to):
        i = len(sends)
        cp = pltpu.make_async_remote_copy(
            src_ref=src, dst_ref=dst, send_sem=ssem.at[i], recv_sem=rsem.at[i],
            device_id=to, device_id_type=MESH,
        )
        cp.start()
        sends.append(cp)
        return cp

    def rows(start, size):
        return pl.ds(pl.multiple_of(start, size), size)

    half = 128 // DP

    def z_exchange(src, mid_a, mid_b, dst_a, dst_b, base):
        a = [send(src.at[i * half : (i + 1) * half], mid_a.at[i * half : (i + 1) * half], at_z(2)) for i in range(DP)]
        b = [send(src.at[128 + i * half : 128 + (i + 1) * half], mid_b.at[i * half : (i + 1) * half], at_z(-2))
             for i in range(DP)]
        last = []
        for i in range(DP):
            rw = slice(i * half, (i + 1) * half)
            yield
            a[i].wait_recv()
            last.append(send(mid_a.at[rw], dst_a.at[rows(base + i * half, half)], at_z(2)))
            yield
            b[i].wait_recv()
            last.append(send(mid_b.at[rw], dst_b.at[rows(base + 128 + i * half, half)], at_z(-2)))
        return last

    def documents():
        c = send(d_ref, dbuf.at[zh, own_p], other)
        below = dbuf.at[lax.div(lax.rem(z + 6, 8), 4)]
        above = dbuf.at[lax.div(lax.rem(z + 2, 8), 4)]
        last = yield from z_exchange(d_ref, dra, drb, below, above, core * 256)
        yield
        c.wait_recv()
        yield
        for cp in last:
            cp.wait_recv()
        e = send(dbuf.at[1 - zh, own_p], dbuf.at[1 - zh, own_p], other)
        yield
        e.wait_recv()
        for fh in range(2):
            for i, part in enumerate(split3(dbuf[fh])):
                ds_[i, fh] = part

    state = {}

    class Chunk:
        def __init__(self, k):
            self.k = k
            self.far = 1 if k % 2 == 0 else -1
            self.to_far, self.to_near = at_y(self.far), at_y(-self.far)
            self.pr, self.pq = k // 2, (k % 2) * 8 * R

        def queries(self):
            k = self.k
            cps = []
            for j in range(2):
                kc = core if j == 0 else 1 - core
                cps.append(send(
                    q_ref.at[rows(64 * kc + R * k, R)],
                    qbuf.at[k, lax.rem(x, 2) * 2 + lax.rem(y, 2), rows(lax.div(y, 2) * R, R),
                            pl.ds(pl.multiple_of(core * 128, 128), 128)],
                    home[j],
                ))
            yield
            for cp in cps:
                cp.wait_recv()
            mine = qbuf.at[k, xo(0), rows(zl * R, R)]
            cps = [send(mine, mine, at_zl(t)) for t in (1, 2, 3)]
            yield
            for cp in cps:
                cp.wait_recv()
            mine = qbuf.at[k, xo(0)]
            cr = send(mine, mine, at_x(1))
            cl = send(mine, mine, at_x(-1))
            yield
            cr.wait_recv()
            part = qbuf.at[k, xo(-1), 0 : 2 * R]
            rr = send(part, part, at_x(1))
            yield
            cl.wait_recv()
            part = qbuf.at[k, xo(1), 2 * R : 4 * R]
            rel = send(part, part, at_x(-1))
            yield
            rr.wait_recv()
            rel.wait_recv()
            for fh in range(2):
                whole = qbuf[k, 2 * fh : 2 * fh + 2].reshape(8 * R, 256)
                for i, part in enumerate(split3(whole)):
                    qs[self.pr, i, fh, self.pq : self.pq + 8 * R, :] = part
            yield

            def scores(i, carry):
                rw = pl.ds(pl.multiple_of(i * 128, 128), 128)
                qw = pl.ds(pl.multiple_of(self.pq + i * 128, 128), 128)
                acc = None
                for a, b in ((2, 0), (1, 1), (0, 2), (1, 0), (0, 1), (0, 0)):
                    for fh in range(2):
                        t = dot_nt(qs[self.pr, a, fh, qw, :], ds_[b, fh])
                        acc = t if acc is None else acc + t
                sbuf[k, rw, :] = acc
                return carry

            lax.fori_loop(0, 8 * R // 128, scores, 0)
            self.cf = send(sbuf.at[k, blk(4 * self.far)], rl.at[k, 0], self.to_far)
            self.cn = send(sbuf.at[k, blk(-3 * self.far)], rs.at[k, 0], self.to_near)

        def reduce_far(self):
            k = self.k
            for s in range(3):
                yield
                self.cf.wait_recv()
                rl[k, s] = rl[k, s] + sbuf[k, blk(self.far * (3 - s)), :]
                self.cf = send(rl.at[k, s], rl.at[k, s + 1], self.to_far)

        def reduce_near(self):
            k = self.k
            for s in range(2):
                yield
                self.cn.wait_recv()
                rs[k, s] = rs[k, s] + sbuf[k, blk(-self.far * (2 - s)), :]
                self.cn = send(rs.at[k, s], rs.at[k, s + 1], self.to_near)

        def join(self):
            k = self.k
            yield
            self.cf.wait_recv()
            self.cn.wait_recv()
            full = (sbuf[k, blk(0), :] + rs[k, 2] + rl[k, 3]) * INV
            sg[k, blk(0), :] = full
            mine = sg.at[k, blk(0)]
            self.af = send(mine, mine, self.to_far)
            self.an = send(mine, mine, self.to_near)
            tc = tcol[rows(64 * core + R * k, R), 0:1]
            top = jnp.max(full, axis=1, keepdims=True)
            total = jnp.sum(jnp.exp(full - top), axis=1, keepdims=True)
            hit = jnp.sum(jnp.where(tc == pidx, full, 0.0), axis=1, keepdims=True)
            ln = lax.broadcasted_iota(jnp.int32, (R, 128), 1)
            pack[k, 0:R, :] = jnp.where(ln == 0, top, jnp.where(ln == 1, total, jnp.where(ln == 2, hit, tc)))
            stx[k, x] = pack[k].T[0:8]
            cps = [send(stx.at[k, x], stx.at[k, x], at_x(t)) for t in (1, 2, 3)]
            yield
            for cp in cps:
                cp.wait_recv()
            stz[k, zl] = tile(*merge(stx[k]))
            cps = [send(stz.at[k, zl], stz.at[k, zl], at_zl(t)) for t in (1, 2, 3)]
            yield
            for cp in cps:
                cp.wait_recv()
            top, total, hit, tgt = merge(stz[k])
            mine = tg.at[k, blk_b(0)]
            tg[k, blk_b(0)] = tile(top + jnp.log(total), hit, tgt, tgt)
            self.g = [send(mine, mine, at_y(t)) for t in range(1, 8)]

        def gather_far(self):
            for s in range(3):
                yield
                self.af.wait_recv()
                part = sg.at[self.k, blk(-self.far * (1 + s))]
                self.af = send(part, part, self.to_far)

        def gather_near(self):
            for s in range(2):
                yield
                self.an.wait_recv()
                part = sg.at[self.k, blk(self.far * (1 + s))]
                self.an = send(part, part, self.to_near)

        def weights(self):
            k, pr, pq = self.k, self.pr, self.pq
            yield
            self.af.wait_recv()
            self.an.wait_recv()
            for cp in self.g:
                cp.wait_recv()
            for b in range(8):
                tpack[k, b : b + 1, :] = tg[k, b, 0:1, :]
                tpack[k, 8 + b : 9 + b, :] = tg[k, b, 2:3, :]
            tt = tpack[k].T
            for b in range(8):
                w = jnp.exp(sg[k, b * R : (b + 1) * R, :] - tt[0:R, b : b + 1])
                w = (w - jnp.where(tt[0:R, 8 + b : 9 + b] == pidx, 1.0, 0.0)) * INV
                w1, w2 = split2(w)
                ws[pr, 0, pq + b * R : pq + (b + 1) * R, :] = w1
                ws[pr, 1, pq + b * R : pq + (b + 1) * R, :] = w2
            if k == K - 1:
                yield
                self.dd_pair(1 - zh)
                state["e0"] = send(dd.at[1 - zh, oth_p], ddr.at[0], other)

            def some(i, carry):
                rw = pl.ds(pl.multiple_of(pq + i * 4 * R, 4 * R), 4 * R)
                for fh in range(2):
                    acc = dot_nn(ws[pr, 1, rw, :], ds_[0, fh])
                    acc = acc + dot_nn(ws[pr, 0, rw, :], ds_[1, fh])
                    dqp[k, 2 * fh + i] = acc + dot_nn(ws[pr, 0, rw, :], ds_[0, fh])
                return carry

            lax.fori_loop(0, 2, some, 0)
            self.ca = send(dqp.at[k, xo(2), 0 : 2 * R], dqa.at[k], at_x(1))
            self.cb = send(dqp.at[k, xo(2), 2 * R : 4 * R], dqb.at[k], at_x(-1))
            self.c1 = send(dqp.at[k, xo(1), 2 * R : 4 * R], dxl.at[k, 2 * R : 4 * R], at_x(1))
            self.c2 = send(dqp.at[k, xo(-1), 0 : 2 * R], dxr.at[k, 0 : 2 * R], at_x(-1))

        def dd_pair(self, fh):
            pr = self.pr
            acc = dot_tn(ws[pr, 1], qs[pr, 0, fh])
            acc = acc + dot_tn(ws[pr, 0], qs[pr, 1, fh])
            acc = acc + dot_tn(ws[pr, 0], qs[pr, 0, fh])
            if pr == 0:
                dd[fh] = acc
            else:
                dd[fh] = dd[fh] + acc

        def documents_term(self):
            yield
            if self.k == K - 1:
                self.dd_pair(zh)
                state["e1"] = send(dd.at[zh, oth_p], ddr.at[1], other)
            elif self.k % 2 == 1:
                self.dd_pair(0)
                self.dd_pair(1)

        def sum_right(self):
            k = self.k
            yield
            self.ca.wait_recv()
            dqa[k] = dqa[k] + dqp[k, xo(1), 0 : 2 * R, :]
            self.c3 = send(dqa.at[k], dxl.at[k, 0 : 2 * R], at_x(1))

        def sum_left(self):
            k = self.k
            yield
            self.cb.wait_recv()
            dqb[k] = dqb[k] + dqp[k, xo(-1), 2 * R : 4 * R, :]
            self.c4 = send(dqb.at[k], dxr.at[k, 2 * R : 4 * R], at_x(-1))

        def sum_join(self):
            k = self.k
            yield
            for cp in (self.c1, self.c2, self.c3, self.c4):
                cp.wait_recv()
            dqt[k] = dqp[k, xo(0)] + dxl[k] + dxr[k]
            cps = [send(dqt.at[k, rows(lax.rem(zl + t, 4) * R, R)], dz.at[k, t - 1], at_zl(t)) for t in (1, 2, 3)]
            yield
            for cp in cps:
                cp.wait_recv()
            mine = rows(zl * R, R)
            dqt[k, mine, :] = dqt[k, mine, :] + dz[k, 0] + dz[k, 1] + dz[k, 2]
            cps = []
            for j in range(2):
                kc = core if j == 0 else 1 - core
                cps.append(send(
                    dqt.at[k, mine, pl.ds(pl.multiple_of(kc * 128, 128), 128)],
                    dqo.at[rows(64 * core + R * k, R)],
                    home[j],
                ))
            yield
            for cp in cps:
                cp.wait_recv()

    sub = lax.broadcasted_iota(jnp.int32, (8, 128), 0)

    def merge(st):
        m = st[:, 0, :]
        top = jnp.max(m, axis=0, keepdims=True)
        total = jnp.sum(st[:, 1, :] * jnp.exp(m - top), axis=0, keepdims=True)
        hit = jnp.sum(st[:, 2, :], axis=0, keepdims=True)
        return top, total, hit, st[0, 3:4, :]

    def tile(a, b, c, d):
        return jnp.where(sub == 0, a, jnp.where(sub == 1, b, jnp.where(sub == 2, c, d)))

    def ending():
        yield
        state["e0"].wait_recv()
        ddt[...] = dd[1 - zh, own_p, :] + ddr[0]
        last = yield from z_exchange(ddt, era, erb, ddz, ddz, 0)
        yield
        state["e1"].wait_recv()
        for cp in last:
            cp.wait_recv()
        dd_ref[...] = dd[zh, own_p, :] + ddr[1] + ddz[...]

    def loss():
        yield
        part = jnp.zeros((8, 128), F32)
        for k in range(K):
            part = part + jnp.where(lane < R, tg[k, :, 0, :] - tg[k, :, 1, :], 0.0)
        lsum[0] = jnp.broadcast_to(jnp.sum(part, keepdims=True), (8, 128))
        cp = send(lsum.at[0], lrecv.at[0], other)
        yield
        cp.wait_recv()
        lsum[1] = lsum[0] + lrecv[0]
        cp = send(lsum.at[1], lrecv.at[1], at_z(4))
        yield
        cp.wait_recv()
        loss_ref[0, 0] = jnp.sum((lsum[1] + lrecv[1])[0:1, 0:1]) * (1.0 / NQ)

    threads = [documents(), ending(), loss()]
    for k in range(K):
        c = Chunk(k)
        threads += [
            c.queries(), c.reduce_far(), c.reduce_near(), c.join(), c.gather_far(), c.gather_near(),
            c.weights(), c.documents_term(), c.sum_right(), c.sum_left(), c.sum_join(),
        ]
    ended = 0
    for t in ORDER:
        if next(threads[t], True):
            ended += 1
    assert ended == len(threads)
    dq_ref[...] = dqo[...]
    for cp in sends:
        cp.wait_send()


def fused(question_vectors, document_vectors, positive):
    vmem = pl.BlockSpec(memory_space=pltpu.VMEM)
    hbm = pl.BlockSpec(memory_space=pltpu.HBM)
    smem = pl.BlockSpec(memory_space=pltpu.SMEM)
    v = pltpu.VMEM
    loss, dq, dd = pl.pallas_call(
        kernel,
        out_shape=(
            jax.ShapeDtypeStruct((1, 1), F32),
            jax.ShapeDtypeStruct((128, 128), F32),
            jax.ShapeDtypeStruct((256, 256), F32),
        ),
        in_specs=[hbm, hbm, hbm],
        out_specs=(smem, vmem, vmem),
        scratch_shapes=[
            v((K, 4, 4 * R, 256), F32),
            v((K // 2, 3, 2, 16 * R, 256), BF16),
            v((2, 512, 256), F32),
            v((3, 2, 512, 256), BF16),
            v((128, 256), F32),
            v((128, 256), F32),
            v((K, 8 * R, 512), F32),
            v((K, 4, R, 512), F32),
            v((K, 3, R, 512), F32),
            v((K, 8 * R, 512), F32),
            v((K // 2, 2, 16 * R, 512), BF16),
            v((128, 128), F32),
            v((K, 128, 128), F32),
            v((K, 128, 128), F32),
            v((K, 4, 8, 128), F32),
            v((K, 4, 8, 128), F32),
            v((K, 8, 8, 128), F32),
            v((K, 4, 4 * R, 256), F32),
            v((K, 2 * R, 256), F32),
            v((K, 2 * R, 256), F32),
            v((K, 4 * R, 256), F32),
            v((K, 4 * R, 256), F32),
            v((K, 3, R, 256), F32),
            v((K, 4 * R, 256), F32),
            v((128, 128), F32),
            v((2, 512, 256), F32),
            v((2, 256, 256), F32),
            v((256, 256), F32),
            v((128, 256), F32),
            v((128, 256), F32),
            v((256, 256), F32),
            v((2, 8, 128), F32),
            v((2, 8, 128), F32),
            v((1, 128), jnp.int32),
            pltpu.SemaphoreType.DMA((N_SEM,)),
            pltpu.SemaphoreType.DMA((N_SEM,)),
            pltpu.SemaphoreType.DMA((2,)),
        ],
        compiler_params=pltpu.CompilerParams(
            collective_id=0, has_side_effects=True, vmem_limit_bytes=40 * 1024 * 1024
        ),
        name="infonce",
    )(question_vectors, document_vectors, positive.reshape(1, 128))
    return loss.reshape(()), dq, dd


def solution(mesh):
    in_specs = (P("row", "col"), P("col", "row"), P("row"))
    out_specs = (P(), P("row", "col"), P("col", "row"))
    return jax.shard_map(fused, mesh=mesh, in_specs=in_specs, out_specs=out_specs, check_vma=False)
```

```python
import jax
import jax.numpy as jnp
from jax import lax
from jax.experimental import pallas as pl
from jax.experimental.pallas import tpu as pltpu
from jax.sharding import PartitionSpec as P

LIST = 4
NQ = 2048
INV = 20.0

K = 4
R = 64 // K
DP = 2
N_SEM = 56 * K + 24
ORDER = (
    0, 1, 3, 4, 5, 6, 7, 8, 11, 12, 13, 15, 16, 17, 18, 19, 22, 23, 24, 26, 27, 28, 29, 30, 33, 34, 35, 37,
    38, 39, 40, 41, 44, 45, 46, 14, 25, 36, 2, 9, 10, 20, 21, 31, 32, 42, 43, 0, 0, 3, 0, 14, 0, 0, 25, 36,
    3, 0, 14, 25, 3, 3, 36, 0, 14, 14, 25, 25, 3, 36, 3, 36, 14, 14, 25, 25, 5, 36, 36, 4, 16, 15, 27, 26,
    38, 37, 6, 17, 28, 7, 8, 6, 18, 19, 39, 17, 30, 29, 28, 40, 41, 39, 9, 20, 31, 10, 11, 12, 21, 42, 22,
    23, 32, 42, 33, 34, 43, 13, 2, 24, 1, 44, 45, 35, 2, 13, 46, 24, 1, 1, 1, 1, 13, 35, 46, 24, 2, 1, 35,
    46,
)

MESH = pl.DeviceIdType.MESH
F32 = jnp.float32
BF16 = jnp.bfloat16


def split2(a):
    hi = a.astype(BF16)
    return hi, (a - hi.astype(F32)).astype(BF16)


def split3(a):
    p1 = a.astype(BF16)
    r1 = a - p1.astype(F32)
    p2 = r1.astype(BF16)
    return p1, p2, (r1 - p2.astype(F32)).astype(BF16)


def dot_nt(a, b):
    return lax.dot_general(a, b, (((1,), (1,)), ((), ())), preferred_element_type=F32)


def dot_nn(a, b):
    return lax.dot_general(a, b, (((1,), (0,)), ((), ())), preferred_element_type=F32)


def dot_tn(a, b):
    return lax.dot_general(a, b, (((0,), (0,)), ((), ())), preferred_element_type=F32)


def kernel(
    q_ref, d_ref, pos_hbm, loss_ref, dq_ref, dd_ref,
    qbuf, qs, dbuf, ds_, dra, drb, sbuf, rl, rs, sg, ws, tcol, pack, tpack,
    stx, tg, dqp, dqa, dqb, dxl, dxr, dz, dqt, dqo,
    dd, ddr, ddt, era, erb, ddz, lsum, lrecv, pos_ref, ssem, rsem, lsem,
):
    row = lax.axis_index("row")
    col = lax.axis_index("col")
    y, zh = lax.div(row, 2), lax.rem(row, 2)
    zl, core = lax.div(col, 8), lax.rem(col, 2)
    x = lax.rem(lax.div(col, 2), 4)
    z = zh * 4 + zl

    def dev(xx, yy, zz, cc):
        return (yy * 2 + lax.div(zz, 4), (lax.rem(zz, 4) * 4 + xx) * 2 + cc)

    def at_y(d):
        return dev(x, lax.rem(y + d + 8, 8), z, core)

    def at_z(d):
        return dev(x, y, lax.rem(z + d + 8, 8), core)

    def at_zl(d):
        return dev(x, y, zh * 4 + lax.rem(zl + d, 4), core)

    def at_x(d):
        return dev(lax.rem(x + d + 4, 4), y, z, core)

    def at_grid(t):
        return dev(lax.rem(x + t % 4, 4), y, zh * 4 + lax.rem(zl + t // 4, 4), core)

    def xi(xx):
        return (1 - lax.rem(xx, 2)) * 2 + lax.div(xx, 2)

    def xo(d):
        return xi(lax.rem(x + d + 4, 4))

    def blk(d):
        yy = lax.rem(y + d + 8, 8)
        b = lax.rem(yy, 2) * 4 + lax.div(yy, 2)
        return pl.ds(pl.multiple_of(b * R, R), R)

    def blk_b(d):
        yy = lax.rem(y + d + 8, 8)
        return lax.rem(yy, 2) * 4 + lax.div(yy, 2)

    other = dev(x, y, z, 1 - core)
    hx = 2 * lax.rem(y, 2) + 1 - lax.rem(x, 2)
    hy = 2 * zl + lax.div(x, 2)
    hz = zh * 4 + lax.div(y, 2)
    home = [dev(hx, hy, hz, core), dev(hx, hy, hz, 1 - core)]

    barrier = pltpu.get_barrier_semaphore()
    partners = [other, at_z(2), at_z(-2), at_z(4)] + [at_y(t) for t in range(1, 8)]
    partners += [at_grid(t) for t in range(1, 16)] + home
    for p in partners:
        pl.semaphore_signal(barrier, inc=1, device_id=p, device_id_type=MESH)

    own_p = pl.ds(pl.multiple_of(core * 256, 256), 256)
    oth_p = pl.ds(pl.multiple_of((1 - core) * 256, 256), 256)
    get_pos = pltpu.make_async_copy(pos_hbm, pos_ref, lsem.at[0])
    get_pos.start()
    get_d = pltpu.make_async_copy(d_ref, dbuf.at[zh, own_p], lsem.at[1])
    get_d.start()
    pack[...] = jnp.zeros_like(pack)
    tpack[...] = jnp.zeros_like(tpack)
    pidx = (512 * (zl * 4 + x) + lax.broadcasted_iota(jnp.int32, (1, 512), 1)).astype(F32)
    lane = lax.broadcasted_iota(jnp.int32, (1, 128), 1)
    get_pos.wait()
    target = (LIST * (row * 128 + lane) + pos_ref[...]).astype(F32)
    tcol[...] = jnp.broadcast_to(target, (128, 128)).T
    get_d.wait()
    pl.semaphore_wait(barrier, len(partners))

    sends = []

    def send(src, dst, to):
        i = len(sends)
        cp = pltpu.make_async_remote_copy(
            src_ref=src, dst_ref=dst, send_sem=ssem.at[i], recv_sem=rsem.at[i],
            device_id=to, device_id_type=MESH,
        )
        cp.start()
        sends.append(cp)
        return cp

    def rows(start, size):
        return pl.ds(pl.multiple_of(start, size), size)

    half = 128 // DP

    def z_exchange(src, mid_a, mid_b, dst_a, dst_b, base):
        a = [send(src.at[i * half : (i + 1) * half], mid_a.at[i * half : (i + 1) * half], at_z(2)) for i in range(DP)]
        b = [send(src.at[128 + i * half : 128 + (i + 1) * half], mid_b.at[i * half : (i + 1) * half], at_z(-2))
             for i in range(DP)]
        last = []
        for i in range(DP):
            rw = slice(i * half, (i + 1) * half)
            yield
            a[i].wait_recv()
            last.append(send(mid_a.at[rw], dst_a.at[rows(base + i * half, half)], at_z(2)))
            yield
            b[i].wait_recv()
            last.append(send(mid_b.at[rw], dst_b.at[rows(base + 128 + i * half, half)], at_z(-2)))
        return last

    def documents():
        c = send(d_ref, dbuf.at[zh, own_p], other)
        below = dbuf.at[lax.div(lax.rem(z + 6, 8), 4)]
        above = dbuf.at[lax.div(lax.rem(z + 2, 8), 4)]
        last = yield from z_exchange(d_ref, dra, drb, below, above, core * 256)
        yield
        c.wait_recv()
        yield
        for cp in last:
            cp.wait_recv()
        e = send(dbuf.at[1 - zh, own_p], dbuf.at[1 - zh, own_p], other)
        yield
        e.wait_recv()
        for fh in range(2):
            for i, part in enumerate(split3(dbuf[fh])):
                ds_[i, fh] = part

    state = {}

    class Chunk:
        def __init__(self, k):
            self.k = k
            self.far = 1 if k % 2 == 0 else -1
            self.pr, self.pq = k // 2, (k % 2) * 8 * R

        def queries(self):
            k = self.k
            cps = []
            for j in range(2):
                kc = core if j == 0 else 1 - core
                cps.append(send(
                    q_ref.at[rows(64 * kc + R * k, R)],
                    qbuf.at[k, lax.rem(x, 2) * 2 + lax.rem(y, 2), rows(lax.div(y, 2) * R, R),
                            pl.ds(pl.multiple_of(core * 128, 128), 128)],
                    home[j],
                ))
            yield
            for cp in cps:
                cp.wait_recv()
            mine = qbuf.at[k, xo(0), rows(zl * R, R)]
            cps = [send(mine, mine, at_zl(t)) for t in (1, 2, 3)]
            yield
            for cp in cps:
                cp.wait_recv()
            mine = qbuf.at[k, xo(0)]
            cr = send(mine, mine, at_x(1))
            cl = send(mine, mine, at_x(-1))
            yield
            cr.wait_recv()
            part = qbuf.at[k, xo(-1), 0 : 2 * R]
            rr = send(part, part, at_x(1))
            yield
            cl.wait_recv()
            part = qbuf.at[k, xo(1), 2 * R : 4 * R]
            rel = send(part, part, at_x(-1))
            yield
            rr.wait_recv()
            rel.wait_recv()
            for fh in range(2):
                whole = qbuf[k, 2 * fh : 2 * fh + 2].reshape(8 * R, 256)
                for i, part in enumerate(split3(whole)):
                    qs[self.pr, i, fh, self.pq : self.pq + 8 * R, :] = part
            yield

            def scores(i, carry):
                rw = pl.ds(pl.multiple_of(i * 128, 128), 128)
                qw = pl.ds(pl.multiple_of(self.pq + i * 128, 128), 128)
                acc = None
                for a, b in ((2, 0), (1, 1), (0, 2), (1, 0), (0, 1), (0, 0)):
                    for fh in range(2):
                        t = dot_nt(qs[self.pr, a, fh, qw, :], ds_[b, fh])
                        acc = t if acc is None else acc + t
                sbuf[k, rw, :] = acc
                return carry

            lax.fori_loop(0, 8 * R // 128, scores, 0)
            f = self.far
            self.m1 = send(sbuf.at[k, blk(4 * f)], rl.at[k, 0], at_y(2 * f))
            self.m2 = send(sbuf.at[k, blk(3 * f)], rl.at[k, 1], at_y(f))
            self.n1 = send(sbuf.at[k, blk(-3 * f)], rs.at[k, 0], at_y(-f))
            self.m4 = send(sbuf.at[k, blk(f)], rl.at[k, 3], at_y(f))
            self.n3 = send(sbuf.at[k, blk(-f)], rs.at[k, 2], at_y(-f))

        def reduce_far(self):
            k, f = self.k, self.far
            yield
            self.m1.wait_recv()
            self.m2.wait_recv()
            rl[k, 0] = rl[k, 0] + rl[k, 1] + sbuf[k, blk(2 * f), :]
            self.m3 = send(rl.at[k, 0], rl.at[k, 2], at_y(2 * f))

        def reduce_near(self):
            k, f = self.k, self.far
            yield
            self.n1.wait_recv()
            rs[k, 0] = rs[k, 0] + sbuf[k, blk(-2 * f), :]
            self.n2 = send(rs.at[k, 0], rs.at[k, 1], at_y(-2 * f))

        def join(self):
            k, f = self.k, self.far
            yield
            for cp in (self.m3, self.m4, self.n2, self.n3):
                cp.wait_recv()
            full = (sbuf[k, blk(0), :] + rs[k, 1] + rs[k, 2] + rl[k, 2] + rl[k, 3]) * INV
            sg[k, blk(0), :] = full
            mine = sg.at[k, blk(0)]
            self.a2 = send(mine, mine, at_y(2 * f))
            self.b2 = send(mine, mine, at_y(-2 * f))
            self.a1 = send(mine, mine, at_y(f))
            self.b1 = send(mine, mine, at_y(-f))
            tc = tcol[rows(64 * core + R * k, R), 0:1]
            top = jnp.max(full, axis=1, keepdims=True)
            total = jnp.sum(jnp.exp(full - top), axis=1, keepdims=True)
            hit = jnp.sum(jnp.where(tc == pidx, full, 0.0), axis=1, keepdims=True)
            ln = lax.broadcasted_iota(jnp.int32, (R, 128), 1)
            pack[k, 0:R, :] = jnp.where(ln == 0, top, jnp.where(ln == 1, total, jnp.where(ln == 2, hit, tc)))
            stx[k, zl * 4 + x] = pack[k].T[0:8]
            mine = stx.at[k, zl * 4 + x]
            cps = [send(mine, mine, at_grid(t)) for t in range(1, 16)]
            yield
            for cp in cps:
                cp.wait_recv()
            top, total, hit, tgt = merge(stx[k])
            mine = tg.at[k, blk_b(0)]
            tg[k, blk_b(0)] = tile(top + jnp.log(total), hit, tgt, tgt)
            self.g = [send(mine, mine, at_y(t)) for t in range(1, 8)]

        def gather_far(self):
            f = self.far
            yield
            self.a2.wait_recv()
            part = sg.at[self.k, blk(-2 * f)]
            self.a4 = send(part, part, at_y(2 * f))
            self.a3 = send(part, part, at_y(f))

        def gather_near(self):
            f = self.far
            yield
            self.b2.wait_recv()
            part = sg.at[self.k, blk(2 * f)]
            self.b3 = send(part, part, at_y(-f))

        def weights(self):
            k, pr, pq = self.k, self.pr, self.pq
            yield
            for cp in [self.a1, self.a3, self.a4, self.b1, self.b3] + self.g:
                cp.wait_recv()
            for b in range(8):
                tpack[k, b : b + 1, :] = tg[k, b, 0:1, :]
                tpack[k, 8 + b : 9 + b, :] = tg[k, b, 2:3, :]
            tt = tpack[k].T
            for b in range(8):
                w = jnp.exp(sg[k, b * R : (b + 1) * R, :] - tt[0:R, b : b + 1])
                w = (w - jnp.where(tt[0:R, 8 + b : 9 + b] == pidx, 1.0, 0.0)) * INV
                w1, w2 = split2(w)
                ws[pr, 0, pq + b * R : pq + (b + 1) * R, :] = w1
                ws[pr, 1, pq + b * R : pq + (b + 1) * R, :] = w2
            if k == K - 1:
                yield
                self.dd_pair(1 - zh)
                state["e0"] = send(dd.at[1 - zh, oth_p], ddr.at[0], other)

            def some(i, carry):
                rw = pl.ds(pl.multiple_of(pq + i * 4 * R, 4 * R), 4 * R)
                for fh in range(2):
                    acc = dot_nn(ws[pr, 1, rw, :], ds_[0, fh])
                    acc = acc + dot_nn(ws[pr, 0, rw, :], ds_[1, fh])
                    dqp[k, 2 * fh + i] = acc + dot_nn(ws[pr, 0, rw, :], ds_[0, fh])
                return carry

            lax.fori_loop(0, 2, some, 0)
            self.ca = send(dqp.at[k, xo(2), 0 : 2 * R], dqa.at[k], at_x(1))
            self.cb = send(dqp.at[k, xo(2), 2 * R : 4 * R], dqb.at[k], at_x(-1))
            self.c1 = send(dqp.at[k, xo(1), 2 * R : 4 * R], dxl.at[k, 2 * R : 4 * R], at_x(1))
            self.c2 = send(dqp.at[k, xo(-1), 0 : 2 * R], dxr.at[k, 0 : 2 * R], at_x(-1))

        def dd_pair(self, fh):
            pr = self.pr
            acc = dot_tn(ws[pr, 1], qs[pr, 0, fh])
            acc = acc + dot_tn(ws[pr, 0], qs[pr, 1, fh])
            acc = acc + dot_tn(ws[pr, 0], qs[pr, 0, fh])
            if pr == 0:
                dd[fh] = acc
            else:
                dd[fh] = dd[fh] + acc

        def documents_term(self):
            yield
            if self.k == K - 1:
                self.dd_pair(zh)
                state["e1"] = send(dd.at[zh, oth_p], ddr.at[1], other)
            elif self.k % 2 == 1:
                self.dd_pair(0)
                self.dd_pair(1)

        def sum_right(self):
            k = self.k
            yield
            self.ca.wait_recv()
            dqa[k] = dqa[k] + dqp[k, xo(1), 0 : 2 * R, :]
            self.c3 = send(dqa.at[k], dxl.at[k, 0 : 2 * R], at_x(1))

        def sum_left(self):
            k = self.k
            yield
            self.cb.wait_recv()
            dqb[k] = dqb[k] + dqp[k, xo(-1), 2 * R : 4 * R, :]
            self.c4 = send(dqb.at[k], dxr.at[k, 2 * R : 4 * R], at_x(-1))

        def sum_join(self):
            k = self.k
            yield
            for cp in (self.c1, self.c2, self.c3, self.c4):
                cp.wait_recv()
            dqt[k] = dqp[k, xo(0)] + dxl[k] + dxr[k]
            cps = [send(dqt.at[k, rows(lax.rem(zl + t, 4) * R, R)], dz.at[k, t - 1], at_zl(t)) for t in (1, 2, 3)]
            yield
            for cp in cps:
                cp.wait_recv()
            mine = rows(zl * R, R)
            dqt[k, mine, :] = dqt[k, mine, :] + dz[k, 0] + dz[k, 1] + dz[k, 2]
            cps = []
            for j in range(2):
                kc = core if j == 0 else 1 - core
                cps.append(send(
                    dqt.at[k, mine, pl.ds(pl.multiple_of(kc * 128, 128), 128)],
                    dqo.at[rows(64 * core + R * k, R)],
                    home[j],
                ))
            yield
            for cp in cps:
                cp.wait_recv()

    sub = lax.broadcasted_iota(jnp.int32, (8, 128), 0)

    def merge(st):
        m = st[:, 0, :]
        top = jnp.max(m, axis=0, keepdims=True)
        total = jnp.sum(st[:, 1, :] * jnp.exp(m - top), axis=0, keepdims=True)
        hit = jnp.sum(st[:, 2, :], axis=0, keepdims=True)
        return top, total, hit, st[0, 3:4, :]

    def tile(a, b, c, d):
        return jnp.where(sub == 0, a, jnp.where(sub == 1, b, jnp.where(sub == 2, c, d)))

    def ending():
        yield
        state["e0"].wait_recv()
        ddt[...] = dd[1 - zh, own_p, :] + ddr[0]
        last = yield from z_exchange(ddt, era, erb, ddz, ddz, 0)
        yield
        state["e1"].wait_recv()
        for cp in last:
            cp.wait_recv()
        dd_ref[...] = dd[zh, own_p, :] + ddr[1] + ddz[...]

    def loss():
        yield
        part = jnp.zeros((8, 128), F32)
        for k in range(K):
            part = part + jnp.where(lane < R, tg[k, :, 0, :] - tg[k, :, 1, :], 0.0)
        lsum[0] = jnp.broadcast_to(jnp.sum(part, keepdims=True), (8, 128))
        cp = send(lsum.at[0], lrecv.at[0], other)
        yield
        cp.wait_recv()
        lsum[1] = lsum[0] + lrecv[0]
        cp = send(lsum.at[1], lrecv.at[1], at_z(4))
        yield
        cp.wait_recv()
        loss_ref[0, 0] = jnp.sum((lsum[1] + lrecv[1])[0:1, 0:1]) * (1.0 / NQ)

    threads = [documents(), ending(), loss()]
    for k in range(K):
        c = Chunk(k)
        threads += [
            c.queries(), c.reduce_far(), c.reduce_near(), c.join(), c.gather_far(), c.gather_near(),
            c.weights(), c.documents_term(), c.sum_right(), c.sum_left(), c.sum_join(),
        ]
    ended = 0
    for t in ORDER:
        if next(threads[t], True):
            ended += 1
    assert ended == len(threads)
    dq_ref[...] = dqo[...]
    for cp in sends:
        cp.wait_send()


def fused(question_vectors, document_vectors, positive):
    vmem = pl.BlockSpec(memory_space=pltpu.VMEM)
    hbm = pl.BlockSpec(memory_space=pltpu.HBM)
    smem = pl.BlockSpec(memory_space=pltpu.SMEM)
    v = pltpu.VMEM
    loss, dq, dd = pl.pallas_call(
        kernel,
        out_shape=(
            jax.ShapeDtypeStruct((1, 1), F32),
            jax.ShapeDtypeStruct((128, 128), F32),
            jax.ShapeDtypeStruct((256, 256), F32),
        ),
        in_specs=[hbm, hbm, hbm],
        out_specs=(smem, vmem, vmem),
        scratch_shapes=[
            v((K, 4, 4 * R, 256), F32),
            v((K // 2, 3, 2, 16 * R, 256), BF16),
            v((2, 512, 256), F32),
            v((3, 2, 512, 256), BF16),
            v((128, 256), F32),
            v((128, 256), F32),
            v((K, 8 * R, 512), F32),
            v((K, 4, R, 512), F32),
            v((K, 3, R, 512), F32),
            v((K, 8 * R, 512), F32),
            v((K // 2, 2, 16 * R, 512), BF16),
            v((128, 128), F32),
            v((K, 128, 128), F32),
            v((K, 128, 128), F32),
            v((K, 16, 8, 128), F32),
            v((K, 8, 8, 128), F32),
            v((K, 4, 4 * R, 256), F32),
            v((K, 2 * R, 256), F32),
            v((K, 2 * R, 256), F32),
            v((K, 4 * R, 256), F32),
            v((K, 4 * R, 256), F32),
            v((K, 3, R, 256), F32),
            v((K, 4 * R, 256), F32),
            v((128, 128), F32),
            v((2, 512, 256), F32),
            v((2, 256, 256), F32),
            v((256, 256), F32),
            v((128, 256), F32),
            v((128, 256), F32),
            v((256, 256), F32),
            v((2, 8, 128), F32),
            v((2, 8, 128), F32),
            v((1, 128), jnp.int32),
            pltpu.SemaphoreType.DMA((N_SEM,)),
            pltpu.SemaphoreType.DMA((N_SEM,)),
            pltpu.SemaphoreType.DMA((2,)),
        ],
        compiler_params=pltpu.CompilerParams(
            collective_id=0, has_side_effects=True, vmem_limit_bytes=40 * 1024 * 1024
        ),
        name="infonce",
    )(question_vectors, document_vectors, positive.reshape(1, 128))
    return loss.reshape(()), dq, dd


def solution(mesh):
    in_specs = (P("row", "col"), P("col", "row"), P("row"))
    out_specs = (P(), P("row", "col"), P("col", "row"))
    return jax.shard_map(fused, mesh=mesh, in_specs=in_specs, out_specs=out_specs, check_vma=False)
```

```python
import jax
import jax.numpy as jnp
from jax import lax
from jax.experimental import pallas as pl
from jax.experimental.pallas import tpu as pltpu
from jax.sharding import PartitionSpec as P

LIST = 4
NQ = 2048
INV = 20.0

K = 4
R = 64 // K
DP = 2
N_SEM = 56 * K + 24
ORDER = (
    0, 1, 3, 4, 5, 6, 7, 8, 11, 12, 13, 15, 16, 17, 18, 19, 22, 23, 24, 26, 27, 28, 29, 30, 33, 34, 35, 37,
    38, 39, 40, 41, 44, 45, 46, 14, 25, 36, 2, 9, 10, 20, 21, 31, 32, 42, 43, 0, 0, 3, 0, 14, 0, 0, 25, 36,
    3, 0, 14, 25, 3, 3, 36, 0, 14, 14, 25, 25, 3, 36, 3, 36, 14, 14, 25, 25, 5, 36, 36, 4, 16, 15, 27, 26,
    38, 37, 6, 17, 28, 7, 8, 6, 18, 19, 39, 17, 30, 29, 28, 40, 41, 39, 9, 20, 31, 10, 11, 12, 21, 42, 22,
    23, 32, 42, 33, 34, 43, 13, 2, 24, 1, 44, 45, 35, 2, 13, 46, 24, 1, 1, 1, 1, 13, 35, 46, 24, 2, 1, 35,
    46,
)

MESH = pl.DeviceIdType.MESH
F32 = jnp.float32
BF16 = jnp.bfloat16


def split2(a):
    hi = a.astype(BF16)
    return hi, (a - hi.astype(F32)).astype(BF16)


def split3(a):
    p1 = a.astype(BF16)
    r1 = a - p1.astype(F32)
    p2 = r1.astype(BF16)
    return p1, p2, (r1 - p2.astype(F32)).astype(BF16)


def dot_nt(a, b):
    return lax.dot_general(a, b, (((1,), (1,)), ((), ())), preferred_element_type=F32)


def dot_nn(a, b):
    return lax.dot_general(a, b, (((1,), (0,)), ((), ())), preferred_element_type=F32)


def kernel(
    q_ref, d_ref, pos_hbm, loss_ref, dq_ref, dd_ref,
    qbuf, qs, dbuf, ds_, dra, drb, sbuf, rl, rs, sg, ws, wts, tcol, pack, tpack,
    stx, tg, dqp, dqa, dqb, dxl, dxr, dz, dqt, dqo,
    dd, ddr, ddt, era, erb, ddz, lsum, lrecv, pos_ref, ssem, rsem, lsem,
):
    row = lax.axis_index("row")
    col = lax.axis_index("col")
    y, zh = lax.div(row, 2), lax.rem(row, 2)
    zl, core = lax.div(col, 8), lax.rem(col, 2)
    x = lax.rem(lax.div(col, 2), 4)
    z = zh * 4 + zl

    def dev(xx, yy, zz, cc):
        return (yy * 2 + lax.div(zz, 4), (lax.rem(zz, 4) * 4 + xx) * 2 + cc)

    def at_y(d):
        return dev(x, lax.rem(y + d + 8, 8), z, core)

    def at_z(d):
        return dev(x, y, lax.rem(z + d + 8, 8), core)

    def at_zl(d):
        return dev(x, y, zh * 4 + lax.rem(zl + d, 4), core)

    def at_x(d):
        return dev(lax.rem(x + d + 4, 4), y, z, core)

    def at_grid(t):
        return dev(lax.rem(x + t % 4, 4), y, zh * 4 + lax.rem(zl + t // 4, 4), core)

    def xi(xx):
        return (1 - lax.rem(xx, 2)) * 2 + lax.div(xx, 2)

    def xo(d):
        return xi(lax.rem(x + d + 4, 4))

    def blk(d):
        yy = lax.rem(y + d + 8, 8)
        b = lax.rem(yy, 2) * 4 + lax.div(yy, 2)
        return pl.ds(pl.multiple_of(b * R, R), R)

    def blk_b(d):
        yy = lax.rem(y + d + 8, 8)
        return lax.rem(yy, 2) * 4 + lax.div(yy, 2)

    other = dev(x, y, z, 1 - core)
    hx = 2 * lax.rem(y, 2) + 1 - lax.rem(x, 2)
    hy = 2 * zl + lax.div(x, 2)
    hz = zh * 4 + lax.div(y, 2)
    home = [dev(hx, hy, hz, core), dev(hx, hy, hz, 1 - core)]

    barrier = pltpu.get_barrier_semaphore()
    partners = [other, at_z(2), at_z(-2), at_z(4)] + [at_y(t) for t in range(1, 8)]
    partners += [at_grid(t) for t in range(1, 16)] + home
    for p in partners:
        pl.semaphore_signal(barrier, inc=1, device_id=p, device_id_type=MESH)

    own_p = pl.ds(pl.multiple_of(core * 256, 256), 256)
    oth_p = pl.ds(pl.multiple_of((1 - core) * 256, 256), 256)
    get_pos = pltpu.make_async_copy(pos_hbm, pos_ref, lsem.at[0])
    get_pos.start()
    get_d = pltpu.make_async_copy(d_ref, dbuf.at[zh, own_p], lsem.at[1])
    get_d.start()
    pack[...] = jnp.zeros_like(pack)
    tpack[...] = jnp.zeros_like(tpack)
    pidx = (512 * (zl * 4 + x) + lax.broadcasted_iota(jnp.int32, (1, 512), 1)).astype(F32)
    lane = lax.broadcasted_iota(jnp.int32, (1, 128), 1)
    get_pos.wait()
    target = (LIST * (row * 128 + lane) + pos_ref[...]).astype(F32)
    tcol[...] = jnp.broadcast_to(target, (128, 128)).T
    get_d.wait()
    pl.semaphore_wait(barrier, len(partners))

    sends = []

    def send(src, dst, to):
        i = len(sends)
        cp = pltpu.make_async_remote_copy(
            src_ref=src, dst_ref=dst, send_sem=ssem.at[i], recv_sem=rsem.at[i],
            device_id=to, device_id_type=MESH,
        )
        cp.start()
        sends.append(cp)
        return cp

    def rows(start, size):
        return pl.ds(pl.multiple_of(start, size), size)

    half = 128 // DP

    def z_exchange(src, mid_a, mid_b, dst_a, dst_b, base):
        a = [send(src.at[i * half : (i + 1) * half], mid_a.at[i * half : (i + 1) * half], at_z(2)) for i in range(DP)]
        b = [send(src.at[128 + i * half : 128 + (i + 1) * half], mid_b.at[i * half : (i + 1) * half], at_z(-2))
             for i in range(DP)]
        last = []
        for i in range(DP):
            rw = slice(i * half, (i + 1) * half)
            yield
            a[i].wait_recv()
            last.append(send(mid_a.at[rw], dst_a.at[rows(base + i * half, half)], at_z(2)))
            yield
            b[i].wait_recv()
            last.append(send(mid_b.at[rw], dst_b.at[rows(base + 128 + i * half, half)], at_z(-2)))
        return last

    def documents():
        c = send(d_ref, dbuf.at[zh, own_p], other)
        below = dbuf.at[lax.div(lax.rem(z + 6, 8), 4)]
        above = dbuf.at[lax.div(lax.rem(z + 2, 8), 4)]
        last = yield from z_exchange(d_ref, dra, drb, below, above, core * 256)
        yield
        c.wait_recv()
        yield
        for cp in last:
            cp.wait_recv()
        e = send(dbuf.at[1 - zh, own_p], dbuf.at[1 - zh, own_p], other)
        yield
        e.wait_recv()
        for fh in range(2):
            for i, part in enumerate(split3(dbuf[fh])):
                ds_[i, fh] = part

    state = {}

    class Chunk:
        def __init__(self, k):
            self.k = k
            self.far = 1 if k % 2 == 0 else -1
            self.pr, self.pq = k // 2, (k % 2) * 8 * R

        def queries(self):
            k = self.k
            cps = []
            for j in range(2):
                kc = core if j == 0 else 1 - core
                cps.append(send(
                    q_ref.at[rows(64 * kc + R * k, R)],
                    qbuf.at[k, lax.rem(x, 2) * 2 + lax.rem(y, 2), rows(lax.div(y, 2) * R, R),
                            pl.ds(pl.multiple_of(core * 128, 128), 128)],
                    home[j],
                ))
            yield
            for cp in cps:
                cp.wait_recv()
            mine = qbuf.at[k, xo(0), rows(zl * R, R)]
            cps = [send(mine, mine, at_zl(t)) for t in (1, 2, 3)]
            yield
            for cp in cps:
                cp.wait_recv()
            mine = qbuf.at[k, xo(0)]
            cr = send(mine, mine, at_x(1))
            cl = send(mine, mine, at_x(-1))
            yield
            cr.wait_recv()
            part = qbuf.at[k, xo(-1), 0 : 2 * R]
            rr = send(part, part, at_x(1))
            yield
            cl.wait_recv()
            part = qbuf.at[k, xo(1), 2 * R : 4 * R]
            rel = send(part, part, at_x(-1))
            yield
            rr.wait_recv()
            rel.wait_recv()
            for fh in range(2):
                whole = qbuf[k, 2 * fh : 2 * fh + 2].reshape(8 * R, 256)
                for i, part in enumerate(split3(whole)):
                    qs[self.pr, i, fh, self.pq : self.pq + 8 * R, :] = part
            yield

            def scores(i, carry):
                rw = pl.ds(pl.multiple_of(i * 128, 128), 128)
                qw = pl.ds(pl.multiple_of(self.pq + i * 128, 128), 128)
                acc = None
                for a, b in ((2, 0), (1, 1), (0, 2), (1, 0), (0, 1), (0, 0)):
                    for fh in range(2):
                        t = dot_nt(qs[self.pr, a, fh, qw, :], ds_[b, fh])
                        acc = t if acc is None else acc + t
                sbuf[k, rw, :] = acc
                return carry

            lax.fori_loop(0, 8 * R // 128, scores, 0)
            f = self.far
            self.m1 = send(sbuf.at[k, blk(4 * f)], rl.at[k, 0], at_y(2 * f))
            self.m2 = send(sbuf.at[k, blk(3 * f)], rl.at[k, 1], at_y(f))
            self.n1 = send(sbuf.at[k, blk(-3 * f)], rs.at[k, 0], at_y(-f))
            self.m4 = send(sbuf.at[k, blk(f)], rl.at[k, 3], at_y(f))
            self.n3 = send(sbuf.at[k, blk(-f)], rs.at[k, 2], at_y(-f))

        def reduce_far(self):
            k, f = self.k, self.far
            yield
            self.m1.wait_recv()
            self.m2.wait_recv()
            rl[k, 0] = rl[k, 0] + rl[k, 1] + sbuf[k, blk(2 * f), :]
            self.m3 = send(rl.at[k, 0], rl.at[k, 2], at_y(2 * f))

        def reduce_near(self):
            k, f = self.k, self.far
            yield
            self.n1.wait_recv()
            rs[k, 0] = rs[k, 0] + sbuf[k, blk(-2 * f), :]
            self.n2 = send(rs.at[k, 0], rs.at[k, 1], at_y(-2 * f))

        def join(self):
            k, f = self.k, self.far
            yield
            for cp in (self.m3, self.m4, self.n2, self.n3):
                cp.wait_recv()
            full = (sbuf[k, blk(0), :] + rs[k, 1] + rs[k, 2] + rl[k, 2] + rl[k, 3]) * INV
            sg[k, blk(0), :] = full
            mine = sg.at[k, blk(0)]
            self.a2 = send(mine, mine, at_y(2 * f))
            self.b2 = send(mine, mine, at_y(-2 * f))
            self.a1 = send(mine, mine, at_y(f))
            self.b1 = send(mine, mine, at_y(-f))
            tc = tcol[rows(64 * core + R * k, R), 0:1]
            top = jnp.max(full, axis=1, keepdims=True)
            total = jnp.sum(jnp.exp(full - top), axis=1, keepdims=True)
            hit = jnp.sum(jnp.where(tc == pidx, full, 0.0), axis=1, keepdims=True)
            ln = lax.broadcasted_iota(jnp.int32, (R, 128), 1)
            pack[k, 0:R, :] = jnp.where(ln == 0, top, jnp.where(ln == 1, total, jnp.where(ln == 2, hit, tc)))
            stx[k, zl * 4 + x] = pack[k].T[0:8]
            mine = stx.at[k, zl * 4 + x]
            cps = [send(mine, mine, at_grid(t)) for t in range(1, 16)]
            yield
            for cp in cps:
                cp.wait_recv()
            top, total, hit, tgt = merge(stx[k])
            mine = tg.at[k, blk_b(0)]
            tg[k, blk_b(0)] = tile(top + jnp.log(total), hit, tgt, tgt)
            self.g = [send(mine, mine, at_y(t)) for t in range(1, 8)]

        def gather_far(self):
            f = self.far
            yield
            self.a2.wait_recv()
            part = sg.at[self.k, blk(-2 * f)]
            self.a4 = send(part, part, at_y(2 * f))
            self.a3 = send(part, part, at_y(f))

        def gather_near(self):
            f = self.far
            yield
            self.b2.wait_recv()
            part = sg.at[self.k, blk(2 * f)]
            self.b3 = send(part, part, at_y(-f))

        def weights(self):
            k, pr, pq = self.k, self.pr, self.pq
            yield
            for cp in [self.a1, self.a3, self.a4, self.b1, self.b3] + self.g:
                cp.wait_recv()
            for b in range(8):
                tpack[k, b : b + 1, :] = tg[k, b, 0:1, :]
                tpack[k, 8 + b : 9 + b, :] = tg[k, b, 2:3, :]
            tt = tpack[k].T
            top = jnp.concatenate([tt[0:R, b : b + 1] for b in range(8)], axis=0)
            tgt = jnp.concatenate([tt[0:R, 8 + b : 9 + b] for b in range(8)], axis=0)
            w = (jnp.exp(sg[k] - top) - jnp.where(tgt == pidx, 1.0, 0.0)) * INV
            for i, part in enumerate(split2(w)):
                ws[pr, i, pq : pq + 8 * R, :] = part
            for i, part in enumerate(split2(w.T)):
                wts[pr, i, :, pq : pq + 8 * R] = part
            if k == K - 1:
                yield
                self.dd_pair(1 - zh)
                state["e0"] = send(dd.at[1 - zh, oth_p], ddr.at[0], other)

            rw = slice(pq, pq + 8 * R)
            for fh in range(2):
                acc = dot_nn(ws[pr, 1, rw, :], ds_[0, fh]) + dot_nn(ws[pr, 0, rw, :], ds_[1, fh])
                acc = acc + dot_nn(ws[pr, 0, rw, :], ds_[0, fh])
                dqp[k, 2 * fh] = acc[0 : 4 * R]
                dqp[k, 2 * fh + 1] = acc[4 * R : 8 * R]
            self.ca = send(dqp.at[k, xo(2), 0 : 2 * R], dqa.at[k], at_x(1))
            self.cb = send(dqp.at[k, xo(2), 2 * R : 4 * R], dqb.at[k], at_x(-1))
            self.c1 = send(dqp.at[k, xo(1), 2 * R : 4 * R], dxl.at[k, 2 * R : 4 * R], at_x(1))
            self.c2 = send(dqp.at[k, xo(-1), 0 : 2 * R], dxr.at[k, 0 : 2 * R], at_x(-1))

        def dd_pair(self, fh):
            pr = self.pr
            acc = dot_nn(wts[pr, 1], qs[pr, 0, fh])
            acc = acc + dot_nn(wts[pr, 0], qs[pr, 1, fh])
            acc = acc + dot_nn(wts[pr, 0], qs[pr, 0, fh])
            if pr == 0:
                dd[fh] = acc
            else:
                dd[fh] = dd[fh] + acc

        def documents_term(self):
            yield
            if self.k == K - 1:
                self.dd_pair(zh)
                state["e1"] = send(dd.at[zh, oth_p], ddr.at[1], other)
            elif self.k % 2 == 1:
                self.dd_pair(0)
                self.dd_pair(1)

        def sum_right(self):
            k = self.k
            yield
            self.ca.wait_recv()
            dqa[k] = dqa[k] + dqp[k, xo(1), 0 : 2 * R, :]
            self.c3 = send(dqa.at[k], dxl.at[k, 0 : 2 * R], at_x(1))

        def sum_left(self):
            k = self.k
            yield
            self.cb.wait_recv()
            dqb[k] = dqb[k] + dqp[k, xo(-1), 2 * R : 4 * R, :]
            self.c4 = send(dqb.at[k], dxr.at[k, 2 * R : 4 * R], at_x(-1))

        def sum_join(self):
            k = self.k
            yield
            for cp in (self.c1, self.c2, self.c3, self.c4):
                cp.wait_recv()
            dqt[k] = dqp[k, xo(0)] + dxl[k] + dxr[k]
            cps = [send(dqt.at[k, rows(lax.rem(zl + t, 4) * R, R)], dz.at[k, t - 1], at_zl(t)) for t in (1, 2, 3)]
            yield
            for cp in cps:
                cp.wait_recv()
            mine = rows(zl * R, R)
            dqt[k, mine, :] = dqt[k, mine, :] + dz[k, 0] + dz[k, 1] + dz[k, 2]
            cps = []
            for j in range(2):
                kc = core if j == 0 else 1 - core
                cps.append(send(
                    dqt.at[k, mine, pl.ds(pl.multiple_of(kc * 128, 128), 128)],
                    dqo.at[rows(64 * core + R * k, R)],
                    home[j],
                ))
            yield
            for cp in cps:
                cp.wait_recv()

    sub = lax.broadcasted_iota(jnp.int32, (8, 128), 0)

    def merge(st):
        m = st[:, 0, :]
        top = jnp.max(m, axis=0, keepdims=True)
        total = jnp.sum(st[:, 1, :] * jnp.exp(m - top), axis=0, keepdims=True)
        hit = jnp.sum(st[:, 2, :], axis=0, keepdims=True)
        return top, total, hit, st[0, 3:4, :]

    def tile(a, b, c, d):
        return jnp.where(sub == 0, a, jnp.where(sub == 1, b, jnp.where(sub == 2, c, d)))

    def ending():
        yield
        state["e0"].wait_recv()
        ddt[...] = dd[1 - zh, own_p, :] + ddr[0]
        last = yield from z_exchange(ddt, era, erb, ddz, ddz, 0)
        yield
        state["e1"].wait_recv()
        for cp in last:
            cp.wait_recv()
        dd_ref[...] = dd[zh, own_p, :] + ddr[1] + ddz[...]

    def loss():
        yield
        part = jnp.zeros((8, 128), F32)
        for k in range(K):
            part = part + jnp.where(lane < R, tg[k, :, 0, :] - tg[k, :, 1, :], 0.0)
        lsum[0] = jnp.broadcast_to(jnp.sum(part, keepdims=True), (8, 128))
        cp = send(lsum.at[0], lrecv.at[0], other)
        yield
        cp.wait_recv()
        lsum[1] = lsum[0] + lrecv[0]
        cp = send(lsum.at[1], lrecv.at[1], at_z(4))
        yield
        cp.wait_recv()
        loss_ref[0, 0] = jnp.sum((lsum[1] + lrecv[1])[0:1, 0:1]) * (1.0 / NQ)

    threads = [documents(), ending(), loss()]
    for k in range(K):
        c = Chunk(k)
        threads += [
            c.queries(), c.reduce_far(), c.reduce_near(), c.join(), c.gather_far(), c.gather_near(),
            c.weights(), c.documents_term(), c.sum_right(), c.sum_left(), c.sum_join(),
        ]
    ended = 0
    for t in ORDER:
        if next(threads[t], True):
            ended += 1
    assert ended == len(threads)
    dq_ref[...] = dqo[...]
    for cp in sends:
        cp.wait_send()


def fused(question_vectors, document_vectors, positive):
    vmem = pl.BlockSpec(memory_space=pltpu.VMEM)
    hbm = pl.BlockSpec(memory_space=pltpu.HBM)
    smem = pl.BlockSpec(memory_space=pltpu.SMEM)
    v = pltpu.VMEM
    loss, dq, dd = pl.pallas_call(
        kernel,
        out_shape=(
            jax.ShapeDtypeStruct((1, 1), F32),
            jax.ShapeDtypeStruct((128, 128), F32),
            jax.ShapeDtypeStruct((256, 256), F32),
        ),
        in_specs=[hbm, hbm, hbm],
        out_specs=(smem, vmem, vmem),
        scratch_shapes=[
            v((K, 4, 4 * R, 256), F32),
            v((K // 2, 3, 2, 16 * R, 256), BF16),
            v((2, 512, 256), F32),
            v((3, 2, 512, 256), BF16),
            v((128, 256), F32),
            v((128, 256), F32),
            v((K, 8 * R, 512), F32),
            v((K, 4, R, 512), F32),
            v((K, 3, R, 512), F32),
            v((K, 8 * R, 512), F32),
            v((K // 2, 2, 16 * R, 512), BF16),
            v((K // 2, 2, 512, 16 * R), BF16),
            v((128, 128), F32),
            v((K, 128, 128), F32),
            v((K, 128, 128), F32),
            v((K, 16, 8, 128), F32),
            v((K, 8, 8, 128), F32),
            v((K, 4, 4 * R, 256), F32),
            v((K, 2 * R, 256), F32),
            v((K, 2 * R, 256), F32),
            v((K, 4 * R, 256), F32),
            v((K, 4 * R, 256), F32),
            v((K, 3, R, 256), F32),
            v((K, 4 * R, 256), F32),
            v((128, 128), F32),
            v((2, 512, 256), F32),
            v((2, 256, 256), F32),
            v((256, 256), F32),
            v((128, 256), F32),
            v((128, 256), F32),
            v((256, 256), F32),
            v((2, 8, 128), F32),
            v((2, 8, 128), F32),
            v((1, 128), jnp.int32),
            pltpu.SemaphoreType.DMA((N_SEM,)),
            pltpu.SemaphoreType.DMA((N_SEM,)),
            pltpu.SemaphoreType.DMA((2,)),
        ],
        compiler_params=pltpu.CompilerParams(
            collective_id=0, has_side_effects=True, vmem_limit_bytes=40 * 1024 * 1024
        ),
        name="infonce",
    )(question_vectors, document_vectors, positive.reshape(1, 128))
    return loss.reshape(()), dq, dd


def solution(mesh):
    in_specs = (P("row", "col"), P("col", "row"), P("row"))
    out_specs = (P(), P("row", "col"), P("col", "row"))
    return jax.shard_map(fused, mesh=mesh, in_specs=in_specs, out_specs=out_specs, check_vma=False)
```

```python
import jax
import jax.numpy as jnp
from jax import lax
from jax.experimental import pallas as pl
from jax.experimental.pallas import tpu as pltpu
from jax.sharding import PartitionSpec as P

LIST = 4
NQ = 2048
INV = 20.0

K = 2
R = 64 // K
DP = 2
N_SEM = 56 * K + 24
ORDER = (
    1, 3, 4, 5, 6, 7, 8, 11, 12, 13, 15, 16, 17, 18, 19, 22, 23, 24, 14, 0, 9, 20, 2, 10, 21, 0, 0, 3, 0, 0,
    0, 14, 3, 0, 14, 0, 3, 3, 14, 14, 3, 3, 14, 14, 5, 4, 16, 15, 6, 17, 6, 7, 8, 17, 18, 19, 9, 20, 10, 20,
    21, 11, 12, 2, 1, 22, 23, 2, 13, 24, 1, 1, 1, 1, 13, 2, 1, 24, 13, 24,
)

MESH = pl.DeviceIdType.MESH
F32 = jnp.float32
BF16 = jnp.bfloat16


def split2(a):
    hi = a.astype(BF16)
    return hi, (a - hi.astype(F32)).astype(BF16)


def split3(a):
    p1 = a.astype(BF16)
    r1 = a - p1.astype(F32)
    p2 = r1.astype(BF16)
    return p1, p2, (r1 - p2.astype(F32)).astype(BF16)


def dot_nt(a, b):
    return lax.dot_general(a, b, (((1,), (1,)), ((), ())), preferred_element_type=F32)


def dot_nn(a, b):
    return lax.dot_general(a, b, (((1,), (0,)), ((), ())), preferred_element_type=F32)


def kernel(
    q_ref, d_ref, pos_hbm, loss_ref, dq_ref, dd_ref,
    qbuf, qs, dbuf, ds_, dra, drb, sbuf, rl, rs, sg, ws, wts, tcol, pack, tpack,
    stx, tg, dqp, dqa, dqb, dxl, dxr, dz, dqt, dqo,
    dd, ddr, ddt, era, erb, ddz, lsum, lrecv, pos_ref, ssem, rsem, lsem,
):
    row = lax.axis_index("row")
    col = lax.axis_index("col")
    y, zh = lax.div(row, 2), lax.rem(row, 2)
    zl, core = lax.div(col, 8), lax.rem(col, 2)
    x = lax.rem(lax.div(col, 2), 4)
    z = zh * 4 + zl

    def dev(xx, yy, zz, cc):
        return (yy * 2 + lax.div(zz, 4), (lax.rem(zz, 4) * 4 + xx) * 2 + cc)

    def at_y(d):
        return dev(x, lax.rem(y + d + 8, 8), z, core)

    def at_z(d):
        return dev(x, y, lax.rem(z + d + 8, 8), core)

    def at_zl(d):
        return dev(x, y, zh * 4 + lax.rem(zl + d, 4), core)

    def at_x(d):
        return dev(lax.rem(x + d + 4, 4), y, z, core)

    def at_grid(t):
        return dev(lax.rem(x + t % 4, 4), y, zh * 4 + lax.rem(zl + t // 4, 4), core)

    def xi(xx):
        return (1 - lax.rem(xx, 2)) * 2 + lax.div(xx, 2)

    def xo(d):
        return xi(lax.rem(x + d + 4, 4))

    def blk(d):
        yy = lax.rem(y + d + 8, 8)
        b = lax.rem(yy, 2) * 4 + lax.div(yy, 2)
        return pl.ds(pl.multiple_of(b * R, R), R)

    def blk_b(d):
        yy = lax.rem(y + d + 8, 8)
        return lax.rem(yy, 2) * 4 + lax.div(yy, 2)

    other = dev(x, y, z, 1 - core)
    hx = 2 * lax.rem(y, 2) + 1 - lax.rem(x, 2)
    hy = 2 * zl + lax.div(x, 2)
    hz = zh * 4 + lax.div(y, 2)
    home = [dev(hx, hy, hz, core), dev(hx, hy, hz, 1 - core)]

    barrier = pltpu.get_barrier_semaphore()
    partners = [other, at_z(2), at_z(-2), at_z(4)] + [at_y(t) for t in range(1, 8)]
    partners += [at_grid(t) for t in range(1, 16)] + home
    for p in partners:
        pl.semaphore_signal(barrier, inc=1, device_id=p, device_id_type=MESH)

    own_p = pl.ds(pl.multiple_of(core * 256, 256), 256)
    oth_p = pl.ds(pl.multiple_of((1 - core) * 256, 256), 256)
    get_pos = pltpu.make_async_copy(pos_hbm, pos_ref, lsem.at[0])
    get_pos.start()
    get_d = pltpu.make_async_copy(d_ref, dbuf.at[zh, own_p], lsem.at[1])
    get_d.start()
    pack[...] = jnp.zeros_like(pack)
    tpack[...] = jnp.zeros_like(tpack)
    pidx = (512 * (zl * 4 + x) + lax.broadcasted_iota(jnp.int32, (1, 512), 1)).astype(F32)
    lane = lax.broadcasted_iota(jnp.int32, (1, 128), 1)
    get_pos.wait()
    target = (LIST * (row * 128 + lane) + pos_ref[...]).astype(F32)
    tcol[...] = jnp.broadcast_to(target, (128, 128)).T
    get_d.wait()
    pl.semaphore_wait(barrier, len(partners))

    sends = []

    def send(src, dst, to):
        i = len(sends)
        cp = pltpu.make_async_remote_copy(
            src_ref=src, dst_ref=dst, send_sem=ssem.at[i], recv_sem=rsem.at[i],
            device_id=to, device_id_type=MESH,
        )
        cp.start()
        sends.append(cp)
        return cp

    def rows(start, size):
        return pl.ds(pl.multiple_of(start, size), size)

    half = 128 // DP

    def z_exchange(src, mid_a, mid_b, dst_a, dst_b, base):
        a = [send(src.at[i * half : (i + 1) * half], mid_a.at[i * half : (i + 1) * half], at_z(2)) for i in range(DP)]
        b = [send(src.at[128 + i * half : 128 + (i + 1) * half], mid_b.at[i * half : (i + 1) * half], at_z(-2))
             for i in range(DP)]
        last = []
        for i in range(DP):
            rw = slice(i * half, (i + 1) * half)
            yield
            a[i].wait_recv()
            last.append(send(mid_a.at[rw], dst_a.at[rows(base + i * half, half)], at_z(2)))
            yield
            b[i].wait_recv()
            last.append(send(mid_b.at[rw], dst_b.at[rows(base + 128 + i * half, half)], at_z(-2)))
        return last

    def documents():
        c = send(d_ref, dbuf.at[zh, own_p], other)
        below = dbuf.at[lax.div(lax.rem(z + 6, 8), 4)]
        above = dbuf.at[lax.div(lax.rem(z + 2, 8), 4)]
        last = yield from z_exchange(d_ref, dra, drb, below, above, core * 256)
        yield
        c.wait_recv()
        yield
        for cp in last:
            cp.wait_recv()
        e = send(dbuf.at[1 - zh, own_p], dbuf.at[1 - zh, own_p], other)
        yield
        e.wait_recv()
        for fh in range(2):
            for i, part in enumerate(split3(dbuf[fh])):
                ds_[i, fh] = part

    state = {}

    class Chunk:
        def __init__(self, k):
            self.k = k
            self.far = 1 if k % 2 == 0 else -1
            self.pr, self.pq = k // 2, (k % 2) * 8 * R

        def queries(self):
            k = self.k
            cps = []
            for j in range(2):
                kc = core if j == 0 else 1 - core
                cps.append(send(
                    q_ref.at[rows(64 * kc + R * k, R)],
                    qbuf.at[k, lax.rem(x, 2) * 2 + lax.rem(y, 2), rows(lax.div(y, 2) * R, R),
                            pl.ds(pl.multiple_of(core * 128, 128), 128)],
                    home[j],
                ))
            yield
            for cp in cps:
                cp.wait_recv()
            mine = qbuf.at[k, xo(0), rows(zl * R, R)]
            cps = [send(mine, mine, at_zl(t)) for t in (1, 2, 3)]
            yield
            for cp in cps:
                cp.wait_recv()
            mine = qbuf.at[k, xo(0)]
            cr = send(mine, mine, at_x(1))
            cl = send(mine, mine, at_x(-1))
            yield
            cr.wait_recv()
            part = qbuf.at[k, xo(-1), 0 : 2 * R]
            rr = send(part, part, at_x(1))
            yield
            cl.wait_recv()
            part = qbuf.at[k, xo(1), 2 * R : 4 * R]
            rel = send(part, part, at_x(-1))
            yield
            rr.wait_recv()
            rel.wait_recv()
            for fh in range(2):
                whole = qbuf[k, 2 * fh : 2 * fh + 2].reshape(8 * R, 256)
                for i, part in enumerate(split3(whole)):
                    qs[self.pr, i, fh, self.pq : self.pq + 8 * R, :] = part
            yield

            def scores(i, carry):
                rw = pl.ds(pl.multiple_of(i * 128, 128), 128)
                qw = pl.ds(pl.multiple_of(self.pq + i * 128, 128), 128)
                acc = None
                for a, b in ((2, 0), (1, 1), (0, 2), (1, 0), (0, 1), (0, 0)):
                    for fh in range(2):
                        t = dot_nt(qs[self.pr, a, fh, qw, :], ds_[b, fh])
                        acc = t if acc is None else acc + t
                sbuf[k, rw, :] = acc
                return carry

            lax.fori_loop(0, 8 * R // 128, scores, 0)
            f = self.far
            self.m1 = send(sbuf.at[k, blk(4 * f)], rl.at[k, 0], at_y(2 * f))
            self.m2 = send(sbuf.at[k, blk(3 * f)], rl.at[k, 1], at_y(f))
            self.n1 = send(sbuf.at[k, blk(-3 * f)], rs.at[k, 0], at_y(-f))
            self.m4 = send(sbuf.at[k, blk(f)], rl.at[k, 3], at_y(f))
            self.n3 = send(sbuf.at[k, blk(-f)], rs.at[k, 2], at_y(-f))

        def reduce_far(self):
            k, f = self.k, self.far
            yield
            self.m1.wait_recv()
            self.m2.wait_recv()
            rl[k, 0] = rl[k, 0] + rl[k, 1] + sbuf[k, blk(2 * f), :]
            self.m3 = send(rl.at[k, 0], rl.at[k, 2], at_y(2 * f))

        def reduce_near(self):
            k, f = self.k, self.far
            yield
            self.n1.wait_recv()
            rs[k, 0] = rs[k, 0] + sbuf[k, blk(-2 * f), :]
            self.n2 = send(rs.at[k, 0], rs.at[k, 1], at_y(-2 * f))

        def join(self):
            k, f = self.k, self.far
            yield
            for cp in (self.m3, self.m4, self.n2, self.n3):
                cp.wait_recv()
            full = (sbuf[k, blk(0), :] + rs[k, 1] + rs[k, 2] + rl[k, 2] + rl[k, 3]) * INV
            sg[k, blk(0), :] = full
            mine = sg.at[k, blk(0)]
            self.a2 = send(mine, mine, at_y(2 * f))
            self.b2 = send(mine, mine, at_y(-2 * f))
            self.a1 = send(mine, mine, at_y(f))
            self.b1 = send(mine, mine, at_y(-f))
            tc = tcol[rows(64 * core + R * k, R), 0:1]
            top = jnp.max(full, axis=1, keepdims=True)
            total = jnp.sum(jnp.exp(full - top), axis=1, keepdims=True)
            hit = jnp.sum(jnp.where(tc == pidx, full, 0.0), axis=1, keepdims=True)
            ln = lax.broadcasted_iota(jnp.int32, (R, 128), 1)
            pack[k, 0:R, :] = jnp.where(ln == 0, top, jnp.where(ln == 1, total, jnp.where(ln == 2, hit, tc)))
            stx[k, zl * 4 + x] = pack[k].T[0:8]
            mine = stx.at[k, zl * 4 + x]
            cps = [send(mine, mine, at_grid(t)) for t in range(1, 16)]
            yield
            for cp in cps:
                cp.wait_recv()
            top, total, hit, tgt = merge(stx[k])
            mine = tg.at[k, blk_b(0)]
            tg[k, blk_b(0)] = tile(top + jnp.log(total), hit, tgt, tgt)
            self.g = [send(mine, mine, at_y(t)) for t in range(1, 8)]

        def gather_far(self):
            f = self.far
            yield
            self.a2.wait_recv()
            part = sg.at[self.k, blk(-2 * f)]
            self.a4 = send(part, part, at_y(2 * f))
            self.a3 = send(part, part, at_y(f))

        def gather_near(self):
            f = self.far
            yield
            self.b2.wait_recv()
            part = sg.at[self.k, blk(2 * f)]
            self.b3 = send(part, part, at_y(-f))

        def weights(self):
            k, pr, pq = self.k, self.pr, self.pq
            yield
            for cp in [self.a1, self.a3, self.a4, self.b1, self.b3] + self.g:
                cp.wait_recv()
            for b in range(8):
                tpack[k, b : b + 1, :] = tg[k, b, 0:1, :]
                tpack[k, 8 + b : 9 + b, :] = tg[k, b, 2:3, :]
            tt = tpack[k].T
            top = jnp.concatenate([tt[0:R, b : b + 1] for b in range(8)], axis=0)
            tgt = jnp.concatenate([tt[0:R, 8 + b : 9 + b] for b in range(8)], axis=0)
            w = (jnp.exp(sg[k] - top) - jnp.where(tgt == pidx, 1.0, 0.0)) * INV
            for i, part in enumerate(split2(w)):
                ws[pr, i, pq : pq + 8 * R, :] = part
            for i, part in enumerate(split2(w.T)):
                wts[pr, i, :, pq : pq + 8 * R] = part
            if k == K - 1:
                yield
                self.dd_pair(1 - zh)
                state["e0"] = send(dd.at[1 - zh, oth_p], ddr.at[0], other)

            rw = slice(pq, pq + 8 * R)
            for fh in range(2):
                acc = dot_nn(ws[pr, 1, rw, :], ds_[0, fh]) + dot_nn(ws[pr, 0, rw, :], ds_[1, fh])
                acc = acc + dot_nn(ws[pr, 0, rw, :], ds_[0, fh])
                dqp[k, 2 * fh] = acc[0 : 4 * R]
                dqp[k, 2 * fh + 1] = acc[4 * R : 8 * R]
            self.ca = send(dqp.at[k, xo(2), 0 : 2 * R], dqa.at[k], at_x(1))
            self.cb = send(dqp.at[k, xo(2), 2 * R : 4 * R], dqb.at[k], at_x(-1))
            self.c1 = send(dqp.at[k, xo(1), 2 * R : 4 * R], dxl.at[k, 2 * R : 4 * R], at_x(1))
            self.c2 = send(dqp.at[k, xo(-1), 0 : 2 * R], dxr.at[k, 0 : 2 * R], at_x(-1))

        def dd_pair(self, fh):
            pr = self.pr
            acc = dot_nn(wts[pr, 1], qs[pr, 0, fh])
            acc = acc + dot_nn(wts[pr, 0], qs[pr, 1, fh])
            acc = acc + dot_nn(wts[pr, 0], qs[pr, 0, fh])
            if pr == 0:
                dd[fh] = acc
            else:
                dd[fh] = dd[fh] + acc

        def documents_term(self):
            yield
            if self.k == K - 1:
                self.dd_pair(zh)
                state["e1"] = send(dd.at[zh, oth_p], ddr.at[1], other)
            elif self.k % 2 == 1:
                self.dd_pair(0)
                self.dd_pair(1)

        def sum_right(self):
            k = self.k
            yield
            self.ca.wait_recv()
            dqa[k] = dqa[k] + dqp[k, xo(1), 0 : 2 * R, :]
            self.c3 = send(dqa.at[k], dxl.at[k, 0 : 2 * R], at_x(1))

        def sum_left(self):
            k = self.k
            yield
            self.cb.wait_recv()
            dqb[k] = dqb[k] + dqp[k, xo(-1), 2 * R : 4 * R, :]
            self.c4 = send(dqb.at[k], dxr.at[k, 2 * R : 4 * R], at_x(-1))

        def sum_join(self):
            k = self.k
            yield
            for cp in (self.c1, self.c2, self.c3, self.c4):
                cp.wait_recv()
            dqt[k] = dqp[k, xo(0)] + dxl[k] + dxr[k]
            cps = [send(dqt.at[k, rows(lax.rem(zl + t, 4) * R, R)], dz.at[k, t - 1], at_zl(t)) for t in (1, 2, 3)]
            yield
            for cp in cps:
                cp.wait_recv()
            mine = rows(zl * R, R)
            dqt[k, mine, :] = dqt[k, mine, :] + dz[k, 0] + dz[k, 1] + dz[k, 2]
            cps = []
            for j in range(2):
                kc = core if j == 0 else 1 - core
                cps.append(send(
                    dqt.at[k, mine, pl.ds(pl.multiple_of(kc * 128, 128), 128)],
                    dqo.at[rows(64 * core + R * k, R)],
                    home[j],
                ))
            yield
            for cp in cps:
                cp.wait_recv()

    sub = lax.broadcasted_iota(jnp.int32, (8, 128), 0)

    def merge(st):
        m = st[:, 0, :]
        top = jnp.max(m, axis=0, keepdims=True)
        total = jnp.sum(st[:, 1, :] * jnp.exp(m - top), axis=0, keepdims=True)
        hit = jnp.sum(st[:, 2, :], axis=0, keepdims=True)
        return top, total, hit, st[0, 3:4, :]

    def tile(a, b, c, d):
        return jnp.where(sub == 0, a, jnp.where(sub == 1, b, jnp.where(sub == 2, c, d)))

    def ending():
        yield
        state["e0"].wait_recv()
        ddt[...] = dd[1 - zh, own_p, :] + ddr[0]
        last = yield from z_exchange(ddt, era, erb, ddz, ddz, 0)
        yield
        state["e1"].wait_recv()
        for cp in last:
            cp.wait_recv()
        dd_ref[...] = dd[zh, own_p, :] + ddr[1] + ddz[...]

    def loss():
        yield
        part = jnp.zeros((8, 128), F32)
        for k in range(K):
            part = part + jnp.where(lane < R, tg[k, :, 0, :] - tg[k, :, 1, :], 0.0)
        lsum[0] = jnp.broadcast_to(jnp.sum(part, keepdims=True), (8, 128))
        cp = send(lsum.at[0], lrecv.at[0], other)
        yield
        cp.wait_recv()
        lsum[1] = lsum[0] + lrecv[0]
        cp = send(lsum.at[1], lrecv.at[1], at_z(4))
        yield
        cp.wait_recv()
        loss_ref[0, 0] = jnp.sum((lsum[1] + lrecv[1])[0:1, 0:1]) * (1.0 / NQ)

    threads = [documents(), ending(), loss()]
    for k in range(K):
        c = Chunk(k)
        threads += [
            c.queries(), c.reduce_far(), c.reduce_near(), c.join(), c.gather_far(), c.gather_near(),
            c.weights(), c.documents_term(), c.sum_right(), c.sum_left(), c.sum_join(),
        ]
    ended = 0
    for t in ORDER:
        if next(threads[t], True):
            ended += 1
    assert ended == len(threads)
    dq_ref[...] = dqo[...]
    for cp in sends:
        cp.wait_send()


def fused(question_vectors, document_vectors, positive):
    vmem = pl.BlockSpec(memory_space=pltpu.VMEM)
    hbm = pl.BlockSpec(memory_space=pltpu.HBM)
    smem = pl.BlockSpec(memory_space=pltpu.SMEM)
    v = pltpu.VMEM
    loss, dq, dd = pl.pallas_call(
        kernel,
        out_shape=(
            jax.ShapeDtypeStruct((1, 1), F32),
            jax.ShapeDtypeStruct((128, 128), F32),
            jax.ShapeDtypeStruct((256, 256), F32),
        ),
        in_specs=[hbm, hbm, hbm],
        out_specs=(smem, vmem, vmem),
        scratch_shapes=[
            v((K, 4, 4 * R, 256), F32),
            v((K // 2, 3, 2, 16 * R, 256), BF16),
            v((2, 512, 256), F32),
            v((3, 2, 512, 256), BF16),
            v((128, 256), F32),
            v((128, 256), F32),
            v((K, 8 * R, 512), F32),
            v((K, 4, R, 512), F32),
            v((K, 3, R, 512), F32),
            v((K, 8 * R, 512), F32),
            v((K // 2, 2, 16 * R, 512), BF16),
            v((K // 2, 2, 512, 16 * R), BF16),
            v((128, 128), F32),
            v((K, 128, 128), F32),
            v((K, 128, 128), F32),
            v((K, 16, 8, 128), F32),
            v((K, 8, 8, 128), F32),
            v((K, 4, 4 * R, 256), F32),
            v((K, 2 * R, 256), F32),
            v((K, 2 * R, 256), F32),
            v((K, 4 * R, 256), F32),
            v((K, 4 * R, 256), F32),
            v((K, 3, R, 256), F32),
            v((K, 4 * R, 256), F32),
            v((128, 128), F32),
            v((2, 512, 256), F32),
            v((2, 256, 256), F32),
            v((256, 256), F32),
            v((128, 256), F32),
            v((128, 256), F32),
            v((256, 256), F32),
            v((2, 8, 128), F32),
            v((2, 8, 128), F32),
            v((1, 128), jnp.int32),
            pltpu.SemaphoreType.DMA((N_SEM,)),
            pltpu.SemaphoreType.DMA((N_SEM,)),
            pltpu.SemaphoreType.DMA((2,)),
        ],
        compiler_params=pltpu.CompilerParams(
            collective_id=0, has_side_effects=True, vmem_limit_bytes=40 * 1024 * 1024
        ),
        name="infonce",
    )(question_vectors, document_vectors, positive.reshape(1, 128))
    return loss.reshape(()), dq, dd


def solution(mesh):
    in_specs = (P("row", "col"), P("col", "row"), P("row"))
    out_specs = (P(), P("row", "col"), P("col", "row"))
    return jax.shard_map(fused, mesh=mesh, in_specs=in_specs, out_specs=out_specs, check_vma=False)
```

```python
import jax
import jax.numpy as jnp
from jax import lax
from jax.experimental import pallas as pl
from jax.experimental.pallas import tpu as pltpu
from jax.sharding import PartitionSpec as P

LIST = 4
NQ = 2048
INV = 20.0

K = 4
R = 64 // K
DP = 2
N_SEM = 56 * K + 24
ORDER = (
    0, 1, 3, 4, 5, 6, 7, 8, 11, 12, 13, 15, 16, 17, 18, 19, 22, 23, 24, 26, 27, 28, 29, 30, 33, 34, 35, 37,
    38, 39, 40, 41, 44, 45, 46, 14, 25, 36, 2, 9, 10, 20, 21, 31, 32, 42, 43, 0, 0, 3, 0, 0, 0, 14, 25, 36,
    3, 0, 14, 3, 3, 25, 0, 36, 14, 3, 14, 25, 3, 25, 36, 14, 36, 14, 5, 4, 25, 25, 16, 36, 36, 15, 27, 6, 26,
    38, 37, 17, 17, 7, 8, 28, 18, 19, 39, 17, 39, 30, 29, 41, 40, 39, 9, 20, 11, 12, 31, 22, 10, 21, 23, 42,
    13, 33, 34, 32, 42, 24, 13, 35, 43, 44, 45, 1, 2, 24, 46, 13, 2, 35, 1, 1, 1, 24, 1, 46, 35, 2, 1, 46,
)

MESH = pl.DeviceIdType.MESH
F32 = jnp.float32
BF16 = jnp.bfloat16


def split2(a):
    hi = a.astype(BF16)
    return hi, (a - hi.astype(F32)).astype(BF16)


def split3(a):
    p1 = a.astype(BF16)
    r1 = a - p1.astype(F32)
    p2 = r1.astype(BF16)
    return p1, p2, (r1 - p2.astype(F32)).astype(BF16)


def dot_nt(a, b):
    return lax.dot_general(a, b, (((1,), (1,)), ((), ())), preferred_element_type=F32)


def dot_nn(a, b):
    return lax.dot_general(a, b, (((1,), (0,)), ((), ())), preferred_element_type=F32)


def kernel(
    q_ref, d_ref, pos_hbm, loss_ref, dq_ref, dd_ref,
    qbuf, qs, dbuf, ds_, dra, drb, sbuf, rl, rs, sg, ws, wts, tcol, pack, tpack,
    stx, tg, dqp, dqa, dqb, dxl, dxr, dz, dqt, dqo,
    dd, ddr, ddt, era, erb, ddz, lsum, lrecv, pos_ref, ssem, rsem, lsem,
):
    row = lax.axis_index("row")
    col = lax.axis_index("col")
    y, zh = lax.div(row, 2), lax.rem(row, 2)
    zl, core = lax.div(col, 8), lax.rem(col, 2)
    x = lax.rem(lax.div(col, 2), 4)
    z = zh * 4 + zl

    def dev(xx, yy, zz, cc):
        return (yy * 2 + lax.div(zz, 4), (lax.rem(zz, 4) * 4 + xx) * 2 + cc)

    def at_y(d):
        return dev(x, lax.rem(y + d + 8, 8), z, core)

    def at_z(d):
        return dev(x, y, lax.rem(z + d + 8, 8), core)

    def at_zl(d):
        return dev(x, y, zh * 4 + lax.rem(zl + d, 4), core)

    def at_x(d):
        return dev(lax.rem(x + d + 4, 4), y, z, core)

    def at_grid(t):
        return dev(lax.rem(x + t % 4, 4), y, zh * 4 + lax.rem(zl + t // 4, 4), core)

    def xi(xx):
        return (1 - lax.rem(xx, 2)) * 2 + lax.div(xx, 2)

    def xo(d):
        return xi(lax.rem(x + d + 4, 4))

    def blk(d):
        yy = lax.rem(y + d + 8, 8)
        b = lax.rem(yy, 2) * 4 + lax.div(yy, 2)
        return pl.ds(pl.multiple_of(b * R, R), R)

    def blk_b(d):
        yy = lax.rem(y + d + 8, 8)
        return lax.rem(yy, 2) * 4 + lax.div(yy, 2)

    other = dev(x, y, z, 1 - core)
    hx = 2 * lax.rem(y, 2) + 1 - lax.rem(x, 2)
    hy = 2 * zl + lax.div(x, 2)
    hz = zh * 4 + lax.div(y, 2)
    home = [dev(hx, hy, hz, core), dev(hx, hy, hz, 1 - core)]

    barrier = pltpu.get_barrier_semaphore()
    partners = [other, at_z(2), at_z(-2), at_z(4)] + [at_y(t) for t in range(1, 8)]
    partners += [at_grid(t) for t in range(1, 16)] + home
    for p in partners:
        pl.semaphore_signal(barrier, inc=1, device_id=p, device_id_type=MESH)

    own_p = pl.ds(pl.multiple_of(core * 256, 256), 256)
    oth_p = pl.ds(pl.multiple_of((1 - core) * 256, 256), 256)
    get_pos = pltpu.make_async_copy(pos_hbm, pos_ref, lsem.at[0])
    get_pos.start()
    get_d = pltpu.make_async_copy(d_ref, dbuf.at[zh, own_p], lsem.at[1])
    get_d.start()
    pack[...] = jnp.zeros_like(pack)
    tpack[...] = jnp.zeros_like(tpack)
    pidx = (512 * (zl * 4 + x) + lax.broadcasted_iota(jnp.int32, (1, 512), 1)).astype(F32)
    lane = lax.broadcasted_iota(jnp.int32, (1, 128), 1)
    get_pos.wait()
    target = (LIST * (row * 128 + lane) + pos_ref[...]).astype(F32)
    tcol[...] = jnp.broadcast_to(target, (128, 128)).T
    get_d.wait()
    pl.semaphore_wait(barrier, len(partners))

    sends = []

    def send(src, dst, to):
        i = len(sends)
        cp = pltpu.make_async_remote_copy(
            src_ref=src, dst_ref=dst, send_sem=ssem.at[i], recv_sem=rsem.at[i],
            device_id=to, device_id_type=MESH,
        )
        cp.start()
        sends.append(cp)
        return cp

    def rows(start, size):
        return pl.ds(pl.multiple_of(start, size), size)

    half = 128 // DP

    def z_exchange(src, mid_a, mid_b, dst_a, dst_b, base):
        a = [send(src.at[i * half : (i + 1) * half], mid_a.at[i * half : (i + 1) * half], at_z(2)) for i in range(DP)]
        b = [send(src.at[128 + i * half : 128 + (i + 1) * half], mid_b.at[i * half : (i + 1) * half], at_z(-2))
             for i in range(DP)]
        last = []
        for i in range(DP):
            rw = slice(i * half, (i + 1) * half)
            yield
            a[i].wait_recv()
            last.append(send(mid_a.at[rw], dst_a.at[rows(base + i * half, half)], at_z(2)))
            yield
            b[i].wait_recv()
            last.append(send(mid_b.at[rw], dst_b.at[rows(base + 128 + i * half, half)], at_z(-2)))
        return last

    def documents():
        c = send(d_ref, dbuf.at[zh, own_p], other)
        below = dbuf.at[lax.div(lax.rem(z + 6, 8), 4)]
        above = dbuf.at[lax.div(lax.rem(z + 2, 8), 4)]
        last = yield from z_exchange(d_ref, dra, drb, below, above, core * 256)
        yield
        c.wait_recv()
        yield
        for cp in last:
            cp.wait_recv()
        e = send(dbuf.at[1 - zh, own_p], dbuf.at[1 - zh, own_p], other)
        yield
        e.wait_recv()
        for fh in range(2):
            for i, part in enumerate(split3(dbuf[fh])):
                ds_[i, fh] = part

    state = {}
    packed = set()
    totals = {}

    class Chunk:
        def __init__(self, k):
            self.k = k
            self.far = 1 if k % 2 == 0 else -1
            self.pr, self.pq = k // 2, (k % 2) * 8 * R

        def queries(self):
            k = self.k
            cps = []
            for j in range(2):
                kc = core if j == 0 else 1 - core
                cps.append(send(
                    q_ref.at[rows(64 * kc + R * k, R)],
                    qbuf.at[k, lax.rem(x, 2) * 2 + lax.rem(y, 2), rows(lax.div(y, 2) * R, R),
                            pl.ds(pl.multiple_of(core * 128, 128), 128)],
                    home[j],
                ))
            yield
            for cp in cps:
                cp.wait_recv()
            mine = qbuf.at[k, xo(0), rows(zl * R, R)]
            cps = [send(mine, mine, at_zl(t)) for t in (1, 2, 3)]
            yield
            for cp in cps:
                cp.wait_recv()
            mine = qbuf.at[k, xo(0)]
            cr = send(mine, mine, at_x(1))
            cl = send(mine, mine, at_x(-1))
            yield
            cr.wait_recv()
            part = qbuf.at[k, xo(-1), 0 : 2 * R]
            rr = send(part, part, at_x(1))
            yield
            cl.wait_recv()
            part = qbuf.at[k, xo(1), 2 * R : 4 * R]
            rel = send(part, part, at_x(-1))
            yield
            rr.wait_recv()
            rel.wait_recv()
            for fh in range(2):
                whole = qbuf[k, 2 * fh : 2 * fh + 2].reshape(8 * R, 256)
                for i, part in enumerate(split3(whole)):
                    qs[self.pr, i, fh, self.pq : self.pq + 8 * R, :] = part
            yield

            def scores(i, carry):
                rw = pl.ds(pl.multiple_of(i * 128, 128), 128)
                qw = pl.ds(pl.multiple_of(self.pq + i * 128, 128), 128)
                acc = None
                for a, b in ((2, 0), (1, 1), (0, 2), (1, 0), (0, 1), (0, 0)):
                    for fh in range(2):
                        t = dot_nt(qs[self.pr, a, fh, qw, :], ds_[b, fh])
                        acc = t if acc is None else acc + t
                sbuf[k, rw, :] = acc
                return carry

            lax.fori_loop(0, 8 * R // 128, scores, 0)
            f = self.far
            self.m1 = send(sbuf.at[k, blk(4 * f)], rl.at[k, 0], at_y(2 * f))
            self.m2 = send(sbuf.at[k, blk(3 * f)], rl.at[k, 1], at_y(f))
            self.n1 = send(sbuf.at[k, blk(-3 * f)], rs.at[k, 0], at_y(-f))
            self.m4 = send(sbuf.at[k, blk(f)], rl.at[k, 3], at_y(f))
            self.n3 = send(sbuf.at[k, blk(-f)], rs.at[k, 2], at_y(-f))

        def reduce_far(self):
            k, f = self.k, self.far
            yield
            self.m1.wait_recv()
            self.m2.wait_recv()
            rl[k, 0] = rl[k, 0] + rl[k, 1] + sbuf[k, blk(2 * f), :]
            self.m3 = send(rl.at[k, 0], rl.at[k, 2], at_y(2 * f))

        def reduce_near(self):
            k, f = self.k, self.far
            yield
            self.n1.wait_recv()
            rs[k, 0] = rs[k, 0] + sbuf[k, blk(-2 * f), :]
            self.n2 = send(rs.at[k, 0], rs.at[k, 1], at_y(-2 * f))

        def join(self):
            k, f = self.k, self.far
            yield
            for cp in (self.m3, self.m4, self.n2, self.n3):
                cp.wait_recv()
            full = (sbuf[k, blk(0), :] + rs[k, 1] + rs[k, 2] + rl[k, 2] + rl[k, 3]) * INV
            sg[k, blk(0), :] = full
            mine = sg.at[k, blk(0)]
            self.a2 = send(mine, mine, at_y(2 * f))
            self.b2 = send(mine, mine, at_y(-2 * f))
            self.a1 = send(mine, mine, at_y(f))
            self.b1 = send(mine, mine, at_y(-f))
            tc = tcol[rows(64 * core + R * k, R), 0:1]
            top = jnp.max(full, axis=1, keepdims=True)
            total = jnp.sum(jnp.exp(full - top), axis=1, keepdims=True)
            hit = jnp.sum(jnp.where(tc == pidx, full, 0.0), axis=1, keepdims=True)
            ln = lax.broadcasted_iota(jnp.int32, (R, 128), 1)
            pr, half = self.pr, (k % 2) * R
            pack[pr, half : half + R, :] = jnp.where(ln == 0, top, jnp.where(ln == 1, total, jnp.where(ln == 2, hit, tc)))
            if k % 2 == 0:
                packed.add(pr)
                return
            yield
            assert pr in packed
            stx[pr, zl * 4 + x] = pack[pr].T[0:8]
            mine = stx.at[pr, zl * 4 + x]
            cps = [send(mine, mine, at_grid(t)) for t in range(1, 16)]
            yield
            for cp in cps:
                cp.wait_recv()
            top, total, hit, tgt = merge(stx[pr])
            mine = tg.at[pr, blk_b(0)]
            tg[pr, blk_b(0)] = tile(top + jnp.log(total), hit, tgt, tgt)
            totals[pr] = [send(mine, mine, at_y(t)) for t in range(1, 8)]

        def gather_far(self):
            f = self.far
            yield
            self.a2.wait_recv()
            part = sg.at[self.k, blk(-2 * f)]
            self.a4 = send(part, part, at_y(2 * f))
            self.a3 = send(part, part, at_y(f))

        def gather_near(self):
            f = self.far
            yield
            self.b2.wait_recv()
            part = sg.at[self.k, blk(2 * f)]
            self.b3 = send(part, part, at_y(-f))

        def weights(self):
            k, pr, pq = self.k, self.pr, self.pq
            yield
            for cp in [self.a1, self.a3, self.a4, self.b1, self.b3] + totals[pr]:
                cp.wait_recv()
            totals[pr] = []
            half = (k % 2) * R
            for b in range(8):
                tpack[k, b : b + 1, :] = tg[pr, b, 0:1, :]
                tpack[k, 8 + b : 9 + b, :] = tg[pr, b, 2:3, :]
            tt = tpack[k].T
            top = jnp.concatenate([tt[half : half + R, b : b + 1] for b in range(8)], axis=0)
            tgt = jnp.concatenate([tt[half : half + R, 8 + b : 9 + b] for b in range(8)], axis=0)
            w = (jnp.exp(sg[k] - top) - jnp.where(tgt == pidx, 1.0, 0.0)) * INV
            for i, part in enumerate(split2(w)):
                ws[pr, i, pq : pq + 8 * R, :] = part
            for i, part in enumerate(split2(w.T)):
                wts[pr, i, :, pq : pq + 8 * R] = part
            if k == K - 1:
                yield
                self.dd_pair(1 - zh)
                state["e0"] = send(dd.at[1 - zh, oth_p], ddr.at[0], other)

            rw = slice(pq, pq + 8 * R)
            for fh in range(2):
                acc = dot_nn(ws[pr, 1, rw, :], ds_[0, fh]) + dot_nn(ws[pr, 0, rw, :], ds_[1, fh])
                acc = acc + dot_nn(ws[pr, 0, rw, :], ds_[0, fh])
                dqp[k, 2 * fh] = acc[0 : 4 * R]
                dqp[k, 2 * fh + 1] = acc[4 * R : 8 * R]
            self.ca = send(dqp.at[k, xo(2), 0 : 2 * R], dqa.at[k], at_x(1))
            self.cb = send(dqp.at[k, xo(2), 2 * R : 4 * R], dqb.at[k], at_x(-1))
            self.c1 = send(dqp.at[k, xo(1), 2 * R : 4 * R], dxl.at[k, 2 * R : 4 * R], at_x(1))
            self.c2 = send(dqp.at[k, xo(-1), 0 : 2 * R], dxr.at[k, 0 : 2 * R], at_x(-1))

        def dd_pair(self, fh):
            pr = self.pr
            acc = dot_nn(wts[pr, 1], qs[pr, 0, fh])
            acc = acc + dot_nn(wts[pr, 0], qs[pr, 1, fh])
            acc = acc + dot_nn(wts[pr, 0], qs[pr, 0, fh])
            if pr == 0:
                dd[fh] = acc
            else:
                dd[fh] = dd[fh] + acc

        def documents_term(self):
            yield
            if self.k == K - 1:
                self.dd_pair(zh)
                state["e1"] = send(dd.at[zh, oth_p], ddr.at[1], other)
            elif self.k % 2 == 1:
                self.dd_pair(0)
                self.dd_pair(1)

        def sum_right(self):
            k = self.k
            yield
            self.ca.wait_recv()
            dqa[k] = dqa[k] + dqp[k, xo(1), 0 : 2 * R, :]
            self.c3 = send(dqa.at[k], dxl.at[k, 0 : 2 * R], at_x(1))

        def sum_left(self):
            k = self.k
            yield
            self.cb.wait_recv()
            dqb[k] = dqb[k] + dqp[k, xo(-1), 2 * R : 4 * R, :]
            self.c4 = send(dqb.at[k], dxr.at[k, 2 * R : 4 * R], at_x(-1))

        def sum_join(self):
            k = self.k
            yield
            for cp in (self.c1, self.c2, self.c3, self.c4):
                cp.wait_recv()
            dqt[k] = dqp[k, xo(0)] + dxl[k] + dxr[k]
            cps = [send(dqt.at[k, rows(lax.rem(zl + t, 4) * R, R)], dz.at[k, t - 1], at_zl(t)) for t in (1, 2, 3)]
            yield
            for cp in cps:
                cp.wait_recv()
            mine = rows(zl * R, R)
            dqt[k, mine, :] = dqt[k, mine, :] + dz[k, 0] + dz[k, 1] + dz[k, 2]
            cps = []
            for j in range(2):
                kc = core if j == 0 else 1 - core
                cps.append(send(
                    dqt.at[k, mine, pl.ds(pl.multiple_of(kc * 128, 128), 128)],
                    dqo.at[rows(64 * core + R * k, R)],
                    home[j],
                ))
            yield
            for cp in cps:
                cp.wait_recv()

    sub = lax.broadcasted_iota(jnp.int32, (8, 128), 0)

    def merge(st):
        m = st[:, 0, :]
        top = jnp.max(m, axis=0, keepdims=True)
        total = jnp.sum(st[:, 1, :] * jnp.exp(m - top), axis=0, keepdims=True)
        hit = jnp.sum(st[:, 2, :], axis=0, keepdims=True)
        return top, total, hit, st[0, 3:4, :]

    def tile(a, b, c, d):
        return jnp.where(sub == 0, a, jnp.where(sub == 1, b, jnp.where(sub == 2, c, d)))

    def ending():
        yield
        state["e0"].wait_recv()
        ddt[...] = dd[1 - zh, own_p, :] + ddr[0]
        last = yield from z_exchange(ddt, era, erb, ddz, ddz, 0)
        yield
        state["e1"].wait_recv()
        for cp in last:
            cp.wait_recv()
        dd_ref[...] = dd[zh, own_p, :] + ddr[1] + ddz[...]

    def loss():
        yield
        part = jnp.zeros((8, 128), F32)
        for pr in range(K // 2):
            part = part + jnp.where(lane < 2 * R, tg[pr, :, 0, :] - tg[pr, :, 1, :], 0.0)
        lsum[0] = jnp.broadcast_to(jnp.sum(part, keepdims=True), (8, 128))
        cp = send(lsum.at[0], lrecv.at[0], other)
        yield
        cp.wait_recv()
        lsum[1] = lsum[0] + lrecv[0]
        cp = send(lsum.at[1], lrecv.at[1], at_z(4))
        yield
        cp.wait_recv()
        loss_ref[0, 0] = jnp.sum((lsum[1] + lrecv[1])[0:1, 0:1]) * (1.0 / NQ)

    threads = [documents(), ending(), loss()]
    for k in range(K):
        c = Chunk(k)
        threads += [
            c.queries(), c.reduce_far(), c.reduce_near(), c.join(), c.gather_far(), c.gather_near(),
            c.weights(), c.documents_term(), c.sum_right(), c.sum_left(), c.sum_join(),
        ]
    ended = 0
    for t in ORDER:
        if next(threads[t], True):
            ended += 1
    assert ended == len(threads)
    dq_ref[...] = dqo[...]
    for cp in sends:
        cp.wait_send()


def fused(question_vectors, document_vectors, positive):
    vmem = pl.BlockSpec(memory_space=pltpu.VMEM)
    hbm = pl.BlockSpec(memory_space=pltpu.HBM)
    smem = pl.BlockSpec(memory_space=pltpu.SMEM)
    v = pltpu.VMEM
    loss, dq, dd = pl.pallas_call(
        kernel,
        out_shape=(
            jax.ShapeDtypeStruct((1, 1), F32),
            jax.ShapeDtypeStruct((128, 128), F32),
            jax.ShapeDtypeStruct((256, 256), F32),
        ),
        in_specs=[hbm, hbm, hbm],
        out_specs=(smem, vmem, vmem),
        scratch_shapes=[
            v((K, 4, 4 * R, 256), F32),
            v((K // 2, 3, 2, 16 * R, 256), BF16),
            v((2, 512, 256), F32),
            v((3, 2, 512, 256), BF16),
            v((128, 256), F32),
            v((128, 256), F32),
            v((K, 8 * R, 512), F32),
            v((K, 4, R, 512), F32),
            v((K, 3, R, 512), F32),
            v((K, 8 * R, 512), F32),
            v((K // 2, 2, 16 * R, 512), BF16),
            v((K // 2, 2, 512, 16 * R), BF16),
            v((128, 128), F32),
            v((K // 2, 128, 128), F32),
            v((K, 128, 128), F32),
            v((K // 2, 16, 8, 128), F32),
            v((K // 2, 8, 8, 128), F32),
            v((K, 4, 4 * R, 256), F32),
            v((K, 2 * R, 256), F32),
            v((K, 2 * R, 256), F32),
            v((K, 4 * R, 256), F32),
            v((K, 4 * R, 256), F32),
            v((K, 3, R, 256), F32),
            v((K, 4 * R, 256), F32),
            v((128, 128), F32),
            v((2, 512, 256), F32),
            v((2, 256, 256), F32),
            v((256, 256), F32),
            v((128, 256), F32),
            v((128, 256), F32),
            v((256, 256), F32),
            v((2, 8, 128), F32),
            v((2, 8, 128), F32),
            v((1, 128), jnp.int32),
            pltpu.SemaphoreType.DMA((N_SEM,)),
            pltpu.SemaphoreType.DMA((N_SEM,)),
            pltpu.SemaphoreType.DMA((2,)),
        ],
        compiler_params=pltpu.CompilerParams(
            collective_id=0, has_side_effects=True, vmem_limit_bytes=40 * 1024 * 1024
        ),
        name="infonce",
    )(question_vectors, document_vectors, positive.reshape(1, 128))
    return loss.reshape(()), dq, dd


def solution(mesh):
    in_specs = (P("row", "col"), P("col", "row"), P("row"))
    out_specs = (P(), P("row", "col"), P("col", "row"))
    return jax.shard_map(fused, mesh=mesh, in_specs=in_specs, out_specs=out_specs, check_vma=False)
```

```python
import jax
import jax.numpy as jnp
from jax import lax
from jax.experimental import pallas as pl
from jax.experimental.pallas import tpu as pltpu
from jax.sharding import PartitionSpec as P

LIST = 4
NQ = 2048
INV = 20.0

K = 2
R = 64 // K
DP = 2
N_SEM = 56 * K + 24
ORDER = (
    1, 3, 4, 6, 8, 5, 11, 7, 12, 13, 15, 16, 18, 19, 22, 23, 24, 14, 17, 0, 2, 9, 20, 10, 21, 0, 0, 3, 0, 0,
    0, 14, 3, 0, 14, 3, 3, 0, 14, 14, 3, 3, 14, 14, 5, 4, 16, 15, 6, 17, 6, 7, 8, 18, 17, 19, 9, 20, 10, 20,
    21, 11, 12, 2, 1, 22, 23, 13, 24, 1, 1, 1, 1, 13, 2, 24, 1, 2, 24, 13,
)

MESH = pl.DeviceIdType.MESH
F32 = jnp.float32
BF16 = jnp.bfloat16


def split2(a):
    hi = a.astype(BF16)
    return hi, (a - hi.astype(F32)).astype(BF16)


def split3(a):
    p1 = a.astype(BF16)
    r1 = a - p1.astype(F32)
    p2 = r1.astype(BF16)
    return p1, p2, (r1 - p2.astype(F32)).astype(BF16)


def dot_nt(a, b):
    return lax.dot_general(a, b, (((1,), (1,)), ((), ())), preferred_element_type=F32)


def dot_nn(a, b):
    return lax.dot_general(a, b, (((1,), (0,)), ((), ())), preferred_element_type=F32)


def kernel(
    q_ref, d_ref, pos_hbm, loss_ref, dq_ref, dd_ref,
    qbuf, qs, dbuf, ds_, dra, drb, sbuf, rl, rs, sg, ws, wts, tcol, pack, tpack,
    stx, tg, dqp, dqa, dqb, dxl, dxr, dz, dqt, dqo,
    dd, ddr, ddt, era, erb, ddz, lsum, lrecv, pos_ref, ssem, rsem, lsem,
):
    row = lax.axis_index("row")
    col = lax.axis_index("col")
    y, zh = lax.div(row, 2), lax.rem(row, 2)
    zl, core = lax.div(col, 8), lax.rem(col, 2)
    x = lax.rem(lax.div(col, 2), 4)
    z = zh * 4 + zl

    def dev(xx, yy, zz, cc):
        return (yy * 2 + lax.div(zz, 4), (lax.rem(zz, 4) * 4 + xx) * 2 + cc)

    def at_y(d):
        return dev(x, lax.rem(y + d + 8, 8), z, core)

    def at_z(d):
        return dev(x, y, lax.rem(z + d + 8, 8), core)

    def at_zl(d):
        return dev(x, y, zh * 4 + lax.rem(zl + d, 4), core)

    def at_x(d):
        return dev(lax.rem(x + d + 4, 4), y, z, core)

    def at_grid(t):
        return dev(lax.rem(x + t % 4, 4), y, zh * 4 + lax.rem(zl + t // 4, 4), core)

    def xi(xx):
        return (1 - lax.rem(xx, 2)) * 2 + lax.div(xx, 2)

    def xo(d):
        return xi(lax.rem(x + d + 4, 4))

    def blk(d):
        yy = lax.rem(y + d + 8, 8)
        b = lax.rem(yy, 2) * 4 + lax.div(yy, 2)
        return pl.ds(pl.multiple_of(b * R, R), R)

    def blk_b(d):
        yy = lax.rem(y + d + 8, 8)
        return lax.rem(yy, 2) * 4 + lax.div(yy, 2)

    other = dev(x, y, z, 1 - core)
    hx = 2 * lax.rem(y, 2) + 1 - lax.rem(x, 2)
    hy = 2 * zl + lax.div(x, 2)
    hz = zh * 4 + lax.div(y, 2)
    home = [dev(hx, hy, hz, core), dev(hx, hy, hz, 1 - core)]

    barrier = pltpu.get_barrier_semaphore()
    partners = [other, at_z(2), at_z(-2), at_z(4)] + [at_y(t) for t in range(1, 8)]
    partners += [at_grid(t) for t in range(1, 16)] + home
    for p in partners:
        pl.semaphore_signal(barrier, inc=1, device_id=p, device_id_type=MESH)

    own_p = pl.ds(pl.multiple_of(core * 256, 256), 256)
    oth_p = pl.ds(pl.multiple_of((1 - core) * 256, 256), 256)
    get_pos = pltpu.make_async_copy(pos_hbm, pos_ref, lsem.at[0])
    get_pos.start()
    get_d = pltpu.make_async_copy(d_ref, dbuf.at[zh, own_p], lsem.at[1])
    get_d.start()
    pack[...] = jnp.zeros_like(pack)
    tpack[...] = jnp.zeros_like(tpack)
    pidx = (512 * (zl * 4 + x) + lax.broadcasted_iota(jnp.int32, (1, 512), 1)).astype(F32)
    lane = lax.broadcasted_iota(jnp.int32, (1, 128), 1)
    get_pos.wait()
    target = (LIST * (row * 128 + lane) + pos_ref[...]).astype(F32)
    tcol[...] = jnp.broadcast_to(target, (128, 128)).T
    get_d.wait()
    pl.semaphore_wait(barrier, len(partners))

    sends = []

    def send(src, dst, to):
        i = len(sends)
        cp = pltpu.make_async_remote_copy(
            src_ref=src, dst_ref=dst, send_sem=ssem.at[i], recv_sem=rsem.at[i],
            device_id=to, device_id_type=MESH,
        )
        cp.start()
        sends.append(cp)
        return cp

    def rows(start, size):
        return pl.ds(pl.multiple_of(start, size), size)

    half = 128 // DP

    def z_exchange(src, mid_a, mid_b, dst_a, dst_b, base):
        a = [send(src.at[i * half : (i + 1) * half], mid_a.at[i * half : (i + 1) * half], at_z(2)) for i in range(DP)]
        b = [send(src.at[128 + i * half : 128 + (i + 1) * half], mid_b.at[i * half : (i + 1) * half], at_z(-2))
             for i in range(DP)]
        last = []
        for i in range(DP):
            rw = slice(i * half, (i + 1) * half)
            yield
            a[i].wait_recv()
            last.append(send(mid_a.at[rw], dst_a.at[rows(base + i * half, half)], at_z(2)))
            yield
            b[i].wait_recv()
            last.append(send(mid_b.at[rw], dst_b.at[rows(base + 128 + i * half, half)], at_z(-2)))
        return last

    def documents():
        c = send(d_ref, dbuf.at[zh, own_p], other)
        below = dbuf.at[lax.div(lax.rem(z + 6, 8), 4)]
        above = dbuf.at[lax.div(lax.rem(z + 2, 8), 4)]
        last = yield from z_exchange(d_ref, dra, drb, below, above, core * 256)
        yield
        c.wait_recv()
        yield
        for cp in last:
            cp.wait_recv()
        e = send(dbuf.at[1 - zh, own_p], dbuf.at[1 - zh, own_p], other)
        yield
        e.wait_recv()
        for fh in range(2):
            for i, part in enumerate(split3(dbuf[fh])):
                ds_[i, fh] = part

    state = {}

    class Chunk:
        def __init__(self, k):
            self.k = k
            self.far = 1 if k % 2 == 0 else -1
            self.pr, self.pq = k // 2, (k % 2) * 8 * R

        def queries(self):
            k = self.k
            cps = []
            for j in range(2):
                kc = core if j == 0 else 1 - core
                cps.append(send(
                    q_ref.at[rows(64 * kc + R * k, R)],
                    qbuf.at[k, lax.rem(x, 2) * 2 + lax.rem(y, 2), rows(lax.div(y, 2) * R, R),
                            pl.ds(pl.multiple_of(core * 128, 128), 128)],
                    home[j],
                ))
            yield
            for cp in cps:
                cp.wait_recv()
            mine = qbuf.at[k, xo(0), rows(zl * R, R)]
            cps = [send(mine, mine, at_zl(t)) for t in (1, 2, 3)]
            yield
            for cp in cps:
                cp.wait_recv()
            mine = qbuf.at[k, xo(0)]
            cr = send(mine, mine, at_x(1))
            cl = send(mine, mine, at_x(-1))
            yield
            cr.wait_recv()
            part = qbuf.at[k, xo(-1), 0 : 2 * R]
            rr = send(part, part, at_x(1))
            yield
            cl.wait_recv()
            part = qbuf.at[k, xo(1), 2 * R : 4 * R]
            rel = send(part, part, at_x(-1))
            yield
            rr.wait_recv()
            rel.wait_recv()
            for fh in range(2):
                whole = qbuf[k, 2 * fh : 2 * fh + 2].reshape(8 * R, 256)
                for i, part in enumerate(split3(whole)):
                    qs[self.pr, i, fh, self.pq : self.pq + 8 * R, :] = part
            yield

            def scores(i, carry):
                rw = pl.ds(pl.multiple_of(i * 128, 128), 128)
                qw = pl.ds(pl.multiple_of(self.pq + i * 128, 128), 128)
                acc = None
                for a, b in ((2, 0), (1, 1), (0, 2), (1, 0), (0, 1), (0, 0)):
                    for fh in range(2):
                        t = dot_nt(qs[self.pr, a, fh, qw, :], ds_[b, fh])
                        acc = t if acc is None else acc + t
                sbuf[k, rw, :] = acc
                return carry

            lax.fori_loop(0, 8 * R // 128, scores, 0)
            f = self.far
            self.m1 = send(sbuf.at[k, blk(4 * f)], rl.at[k, 0], at_y(2 * f))
            self.m2 = send(sbuf.at[k, blk(3 * f)], rl.at[k, 1], at_y(f))
            self.n1 = send(sbuf.at[k, blk(-3 * f)], rs.at[k, 0], at_y(-f))
            self.m4 = send(sbuf.at[k, blk(f)], rl.at[k, 3], at_y(f))
            self.n3 = send(sbuf.at[k, blk(-f)], rs.at[k, 2], at_y(-f))

        def reduce_far(self):
            k, f = self.k, self.far
            yield
            self.m1.wait_recv()
            self.m2.wait_recv()
            rl[k, 0] = rl[k, 0] + rl[k, 1] + sbuf[k, blk(2 * f), :]
            self.m3 = send(rl.at[k, 0], rl.at[k, 2], at_y(2 * f))

        def reduce_near(self):
            k, f = self.k, self.far
            yield
            self.n1.wait_recv()
            rs[k, 0] = rs[k, 0] + sbuf[k, blk(-2 * f), :]
            self.n2 = send(rs.at[k, 0], rs.at[k, 1], at_y(-2 * f))

        def join(self):
            k, f = self.k, self.far
            yield
            for cp in (self.m3, self.m4, self.n2, self.n3):
                cp.wait_recv()
            full = (sbuf[k, blk(0), :] + rs[k, 1] + rs[k, 2] + rl[k, 2] + rl[k, 3]) * INV
            sg[k, blk(0), :] = full
            mine = sg.at[k, blk(0)]
            self.a2 = send(mine, mine, at_y(2 * f))
            self.b2 = send(mine, mine, at_y(-2 * f))
            self.a1 = send(mine, mine, at_y(f))
            self.b1 = send(mine, mine, at_y(-f))
            tc = tcol[rows(64 * core + R * k, R), 0:1]
            top = jnp.max(full, axis=1, keepdims=True)
            total = jnp.sum(jnp.exp(full - top), axis=1, keepdims=True)
            hit = jnp.sum(jnp.where(tc == pidx, full, 0.0), axis=1, keepdims=True)
            ln = lax.broadcasted_iota(jnp.int32, (R, 128), 1)
            pack[k, 0:R, :] = jnp.where(ln == 0, top, jnp.where(ln == 1, total, jnp.where(ln == 2, hit, tc)))
            stx[k, zl * 4 + x] = pack[k].T[0:8]
            mine = stx.at[k, zl * 4 + x]
            cps = [send(mine, mine, at_grid(t)) for t in range(1, 16)]
            yield
            for cp in cps:
                cp.wait_recv()
            top, total, hit, tgt = merge(stx[k])
            mine = tg.at[k, blk_b(0)]
            tg[k, blk_b(0)] = tile(top + jnp.log(total), hit, tgt, tgt)
            self.g = [send(mine, mine, at_y(t)) for t in range(1, 8)]

        def gather_far(self):
            f = self.far
            yield
            self.a2.wait_recv()
            part = sg.at[self.k, blk(-2 * f)]
            self.a4 = send(part, part, at_y(2 * f))
            self.a3 = send(part, part, at_y(f))

        def gather_near(self):
            f = self.far
            yield
            self.b2.wait_recv()
            part = sg.at[self.k, blk(2 * f)]
            self.b3 = send(part, part, at_y(-f))

        def weights(self):
            k, pr, pq = self.k, self.pr, self.pq
            yield
            for cp in [self.a1, self.a3, self.a4, self.b1, self.b3] + self.g:
                cp.wait_recv()
            for b in range(8):
                tpack[k, b : b + 1, :] = tg[k, b, 0:1, :]
                tpack[k, 8 + b : 9 + b, :] = tg[k, b, 2:3, :]
            tt = tpack[k].T
            top = jnp.concatenate([tt[0:R, b : b + 1] for b in range(8)], axis=0)
            tgt = jnp.concatenate([tt[0:R, 8 + b : 9 + b] for b in range(8)], axis=0)
            w = (jnp.exp(sg[k] - top) - jnp.where(tgt == pidx, 1.0, 0.0)) * INV
            for i, part in enumerate(split2(w)):
                ws[pr, i, pq : pq + 8 * R, :] = part
            for i, part in enumerate(split2(w.T)):
                wts[pr, i, :, pq : pq + 8 * R] = part
            if k == K - 1:
                yield
                self.dd_pair(1 - zh)
                state["e0"] = send(dd.at[1 - zh, oth_p], ddr.at[0], other)

            rw = slice(pq, pq + 8 * R)
            for fh in range(2):
                acc = dot_nn(ws[pr, 1, rw, :], ds_[0, fh]) + dot_nn(ws[pr, 0, rw, :], ds_[1, fh])
                acc = acc + dot_nn(ws[pr, 0, rw, :], ds_[0, fh])
                dqp[k, 2 * fh] = acc[0 : 4 * R]
                dqp[k, 2 * fh + 1] = acc[4 * R : 8 * R]
            self.ca = send(dqp.at[k, xo(2), 0 : 2 * R], dqa.at[k], at_x(1))
            self.cb = send(dqp.at[k, xo(2), 2 * R : 4 * R], dqb.at[k], at_x(-1))
            self.c1 = send(dqp.at[k, xo(1), 2 * R : 4 * R], dxl.at[k, 2 * R : 4 * R], at_x(1))
            self.c2 = send(dqp.at[k, xo(-1), 0 : 2 * R], dxr.at[k, 0 : 2 * R], at_x(-1))

        def dd_pair(self, fh):
            pr = self.pr
            acc = dot_nn(wts[pr, 1], qs[pr, 0, fh])
            acc = acc + dot_nn(wts[pr, 0], qs[pr, 1, fh])
            acc = acc + dot_nn(wts[pr, 0], qs[pr, 0, fh])
            if pr == 0:
                dd[fh] = acc
            else:
                dd[fh] = dd[fh] + acc

        def documents_term(self):
            yield
            if self.k == K - 1:
                self.dd_pair(zh)
                state["e1"] = send(dd.at[zh, oth_p], ddr.at[1], other)
            elif self.k % 2 == 1:
                self.dd_pair(0)
                self.dd_pair(1)

        def sum_right(self):
            k = self.k
            yield
            self.ca.wait_recv()
            dqa[k] = dqa[k] + dqp[k, xo(1), 0 : 2 * R, :]
            self.c3 = send(dqa.at[k], dxl.at[k, 0 : 2 * R], at_x(1))

        def sum_left(self):
            k = self.k
            yield
            self.cb.wait_recv()
            dqb[k] = dqb[k] + dqp[k, xo(-1), 2 * R : 4 * R, :]
            self.c4 = send(dqb.at[k], dxr.at[k, 2 * R : 4 * R], at_x(-1))

        def sum_join(self):
            k = self.k
            yield
            for cp in (self.c1, self.c2, self.c3, self.c4):
                cp.wait_recv()
            dqt[k] = dqp[k, xo(0)] + dxl[k] + dxr[k]
            cps = [send(dqt.at[k, rows(lax.rem(zl + t, 4) * R, R)], dz.at[k, t - 1], at_zl(t)) for t in (1, 2, 3)]
            yield
            for cp in cps:
                cp.wait_recv()
            mine = rows(zl * R, R)
            dqt[k, mine, :] = dqt[k, mine, :] + dz[k, 0] + dz[k, 1] + dz[k, 2]
            cps = []
            for j in range(2):
                kc = core if j == 0 else 1 - core
                cps.append(send(
                    dqt.at[k, mine, pl.ds(pl.multiple_of(kc * 128, 128), 128)],
                    dqo.at[rows(64 * core + R * k, R)],
                    home[j],
                ))
            yield
            for cp in cps:
                cp.wait_recv()

    sub = lax.broadcasted_iota(jnp.int32, (8, 128), 0)

    def merge(st):
        m = st[:, 0, :]
        top = jnp.max(m, axis=0, keepdims=True)
        total = jnp.sum(st[:, 1, :] * jnp.exp(m - top), axis=0, keepdims=True)
        hit = jnp.sum(st[:, 2, :], axis=0, keepdims=True)
        return top, total, hit, st[0, 3:4, :]

    def tile(a, b, c, d):
        return jnp.where(sub == 0, a, jnp.where(sub == 1, b, jnp.where(sub == 2, c, d)))

    def ending():
        yield
        state["e0"].wait_recv()
        ddt[...] = dd[1 - zh, own_p, :] + ddr[0]
        last = yield from z_exchange(ddt, era, erb, ddz, ddz, 0)
        yield
        state["e1"].wait_recv()
        for cp in last:
            cp.wait_recv()
        dd_ref[...] = dd[zh, own_p, :] + ddr[1] + ddz[...]

    def loss():
        yield
        part = jnp.zeros((8, 128), F32)
        for k in range(K):
            part = part + jnp.where(lane < R, tg[k, :, 0, :] - tg[k, :, 1, :], 0.0)
        lsum[0] = jnp.broadcast_to(jnp.sum(part, keepdims=True), (8, 128))
        cp = send(lsum.at[0], lrecv.at[0], other)
        yield
        cp.wait_recv()
        lsum[1] = lsum[0] + lrecv[0]
        cp = send(lsum.at[1], lrecv.at[1], at_z(4))
        yield
        cp.wait_recv()
        loss_ref[0, 0] = jnp.sum((lsum[1] + lrecv[1])[0:1, 0:1]) * (1.0 / NQ)

    threads = [documents(), ending(), loss()]
    for k in range(K):
        c = Chunk(k)
        threads += [
            c.queries(), c.reduce_far(), c.reduce_near(), c.join(), c.gather_far(), c.gather_near(),
            c.weights(), c.documents_term(), c.sum_right(), c.sum_left(), c.sum_join(),
        ]
    ended = 0
    for t in ORDER:
        if next(threads[t], True):
            ended += 1
    assert ended == len(threads)
    dq_ref[...] = dqo[...]
    for cp in sends:
        cp.wait_send()


def fused(question_vectors, document_vectors, positive):
    vmem = pl.BlockSpec(memory_space=pltpu.VMEM)
    hbm = pl.BlockSpec(memory_space=pltpu.HBM)
    smem = pl.BlockSpec(memory_space=pltpu.SMEM)
    v = pltpu.VMEM
    loss, dq, dd = pl.pallas_call(
        kernel,
        out_shape=(
            jax.ShapeDtypeStruct((1, 1), F32),
            jax.ShapeDtypeStruct((128, 128), F32),
            jax.ShapeDtypeStruct((256, 256), F32),
        ),
        in_specs=[hbm, hbm, hbm],
        out_specs=(smem, vmem, vmem),
        scratch_shapes=[
            v((K, 4, 4 * R, 256), F32),
            v((K // 2, 3, 2, 16 * R, 256), BF16),
            v((2, 512, 256), F32),
            v((3, 2, 512, 256), BF16),
            v((128, 256), F32),
            v((128, 256), F32),
            v((K, 8 * R, 512), F32),
            v((K, 4, R, 512), F32),
            v((K, 3, R, 512), F32),
            v((K, 8 * R, 512), F32),
            v((K // 2, 2, 16 * R, 512), BF16),
            v((K // 2, 2, 512, 16 * R), BF16),
            v((128, 128), F32),
            v((K, 128, 128), F32),
            v((K, 128, 128), F32),
            v((K, 16, 8, 128), F32),
            v((K, 8, 8, 128), F32),
            v((K, 4, 4 * R, 256), F32),
            v((K, 2 * R, 256), F32),
            v((K, 2 * R, 256), F32),
            v((K, 4 * R, 256), F32),
            v((K, 4 * R, 256), F32),
            v((K, 3, R, 256), F32),
            v((K, 4 * R, 256), F32),
            v((128, 128), F32),
            v((2, 512, 256), F32),
            v((2, 256, 256), F32),
            v((256, 256), F32),
            v((128, 256), F32),
            v((128, 256), F32),
            v((256, 256), F32),
            v((2, 8, 128), F32),
            v((2, 8, 128), F32),
            v((1, 128), jnp.int32),
            pltpu.SemaphoreType.DMA((N_SEM,)),
            pltpu.SemaphoreType.DMA((N_SEM,)),
            pltpu.SemaphoreType.DMA((2,)),
        ],
        compiler_params=pltpu.CompilerParams(
            collective_id=0, has_side_effects=True, vmem_limit_bytes=40 * 1024 * 1024
        ),
        name="infonce",
    )(question_vectors, document_vectors, positive.reshape(1, 128))
    return loss.reshape(()), dq, dd


def solution(mesh):
    in_specs = (P("row", "col"), P("col", "row"), P("row"))
    out_specs = (P(), P("row", "col"), P("col", "row"))
    return jax.shard_map(fused, mesh=mesh, in_specs=in_specs, out_specs=out_specs, check_vma=False)
```

```python
import jax
import jax.numpy as jnp
from jax import lax
from jax.experimental import pallas as pl
from jax.experimental.pallas import tpu as pltpu
from jax.sharding import PartitionSpec as P

LIST = 4
NQ = 2048
INV = 20.0

K = 2
R = 64 // K
DP = 2
N_SEM = 56 * K + 24
ORDER = (
    3, 4, 1, 6, 8, 5, 11, 7, 12, 13, 15, 16, 18, 19, 0, 23, 24, 14, 17, 20, 2, 9, 10, 21, 0, 22, 0, 3, 0, 0,
    0, 14, 3, 0, 3, 14, 3, 0, 14, 14, 3, 3, 14, 14, 5, 4, 16, 15, 6, 17, 8, 6, 7, 18, 17, 19, 9, 20, 10, 20,
    21, 11, 12, 1, 2, 22, 23, 13, 24, 1, 1, 13, 1, 1, 2, 24, 1, 2, 24, 13,
)

MESH = pl.DeviceIdType.MESH
F32 = jnp.float32
BF16 = jnp.bfloat16


def split2(a):
    hi = a.astype(BF16)
    return hi, (a - hi.astype(F32)).astype(BF16)


def split3(a):
    p1 = a.astype(BF16)
    r1 = a - p1.astype(F32)
    p2 = r1.astype(BF16)
    return p1, p2, (r1 - p2.astype(F32)).astype(BF16)


def dot_nt(a, b):
    return lax.dot_general(a, b, (((1,), (1,)), ((), ())), preferred_element_type=F32)


def dot_nn(a, b):
    return lax.dot_general(a, b, (((1,), (0,)), ((), ())), preferred_element_type=F32)


def kernel(
    q_ref, d_ref, pos_hbm, loss_ref, dq_ref, dd_ref,
    qbuf, qs, dbuf, ds_, dra, drb, sbuf, rl, rs, sg, ws, wts, tcol, pack, tpack,
    stx, tg, dqp, dqa, dqb, dxl, dxr, dz, dqt, dqo,
    dd, ddr, ddt, era, erb, ddz, lsum, lrecv, pos_ref, ssem, rsem, lsem,
):
    row = lax.axis_index("row")
    col = lax.axis_index("col")
    y, zh = lax.div(row, 2), lax.rem(row, 2)
    zl, core = lax.div(col, 8), lax.rem(col, 2)
    x = lax.rem(lax.div(col, 2), 4)
    z = zh * 4 + zl

    def dev(xx, yy, zz, cc):
        return (yy * 2 + lax.div(zz, 4), (lax.rem(zz, 4) * 4 + xx) * 2 + cc)

    def at_y(d):
        return dev(x, lax.rem(y + d + 8, 8), z, core)

    def at_z(d):
        return dev(x, y, lax.rem(z + d + 8, 8), core)

    def at_zl(d):
        return dev(x, y, zh * 4 + lax.rem(zl + d, 4), core)

    def at_x(d):
        return dev(lax.rem(x + d + 4, 4), y, z, core)

    def at_grid(t):
        return dev(lax.rem(x + t % 4, 4), y, zh * 4 + lax.rem(zl + t // 4, 4), core)

    def xi(xx):
        return (1 - lax.rem(xx, 2)) * 2 + lax.div(xx, 2)

    def xo(d):
        return xi(lax.rem(x + d + 4, 4))

    def blk(d):
        yy = lax.rem(y + d + 8, 8)
        b = lax.rem(yy, 2) * 4 + lax.div(yy, 2)
        return pl.ds(pl.multiple_of(b * R, R), R)

    def blk_b(d):
        yy = lax.rem(y + d + 8, 8)
        return lax.rem(yy, 2) * 4 + lax.div(yy, 2)

    other = dev(x, y, z, 1 - core)
    hx = 2 * lax.rem(y, 2) + 1 - lax.rem(x, 2)
    hy = 2 * zl + lax.div(x, 2)
    hz = zh * 4 + lax.div(y, 2)
    home = [dev(hx, hy, hz, core), dev(hx, hy, hz, 1 - core)]

    barrier = pltpu.get_barrier_semaphore()
    partners = [other, at_z(2), at_z(-2), at_z(4)] + [at_y(t) for t in range(1, 8)]
    partners += [at_grid(t) for t in range(1, 16)] + home
    for p in partners:
        pl.semaphore_signal(barrier, inc=1, device_id=p, device_id_type=MESH)

    own_p = pl.ds(pl.multiple_of(core * 256, 256), 256)
    oth_p = pl.ds(pl.multiple_of((1 - core) * 256, 256), 256)
    get_pos = pltpu.make_async_copy(pos_hbm, pos_ref, lsem.at[0])
    get_pos.start()
    get_d = pltpu.make_async_copy(d_ref, dbuf.at[zh, own_p], lsem.at[1])
    get_d.start()
    pack[...] = jnp.zeros_like(pack)
    tpack[...] = jnp.zeros_like(tpack)
    pidx = (512 * (zl * 4 + x) + lax.broadcasted_iota(jnp.int32, (1, 512), 1)).astype(F32)
    lane = lax.broadcasted_iota(jnp.int32, (1, 128), 1)
    get_pos.wait()
    target = (LIST * (row * 128 + lane) + pos_ref[...]).astype(F32)
    tcol[...] = jnp.broadcast_to(target, (128, 128)).T
    get_d.wait()
    pl.semaphore_wait(barrier, len(partners))

    sends = []

    def send(src, dst, to):
        i = len(sends)
        cp = pltpu.make_async_remote_copy(
            src_ref=src, dst_ref=dst, send_sem=ssem.at[i], recv_sem=rsem.at[i],
            device_id=to, device_id_type=MESH,
        )
        cp.start()
        sends.append(cp)
        return cp

    def rows(start, size):
        return pl.ds(pl.multiple_of(start, size), size)

    half = 128 // DP

    def z_exchange(src, mid_a, mid_b, dst_a, dst_b, base):
        a = [send(src.at[i * half : (i + 1) * half], mid_a.at[i * half : (i + 1) * half], at_z(2)) for i in range(DP)]
        b = [send(src.at[128 + i * half : 128 + (i + 1) * half], mid_b.at[i * half : (i + 1) * half], at_z(-2))
             for i in range(DP)]
        last = []
        for i in range(DP):
            rw = slice(i * half, (i + 1) * half)
            yield
            a[i].wait_recv()
            last.append(send(mid_a.at[rw], dst_a.at[rows(base + i * half, half)], at_z(2)))
            yield
            b[i].wait_recv()
            last.append(send(mid_b.at[rw], dst_b.at[rows(base + 128 + i * half, half)], at_z(-2)))
        return last

    def documents():
        c = send(d_ref, dbuf.at[zh, own_p], other)
        below = dbuf.at[lax.div(lax.rem(z + 6, 8), 4)]
        above = dbuf.at[lax.div(lax.rem(z + 2, 8), 4)]
        last = yield from z_exchange(d_ref, dra, drb, below, above, core * 256)
        yield
        c.wait_recv()
        yield
        for cp in last:
            cp.wait_recv()
        e = send(dbuf.at[1 - zh, own_p], dbuf.at[1 - zh, own_p], other)
        yield
        e.wait_recv()
        for fh in range(2):
            for i, part in enumerate(split3(dbuf[fh])):
                ds_[i, fh] = part

    state = {}

    class Chunk:
        def __init__(self, k):
            self.k = k
            self.far = 1 if k % 2 == 0 else -1
            self.pr, self.pq = k // 2, (k % 2) * 8 * R

        def queries(self):
            k = self.k
            cps = []
            for j in range(2):
                kc = core if j == 0 else 1 - core
                cps.append(send(
                    q_ref.at[rows(64 * kc + R * k, R)],
                    qbuf.at[k, lax.rem(x, 2) * 2 + lax.rem(y, 2), rows(lax.div(y, 2) * R, R),
                            pl.ds(pl.multiple_of(core * 128, 128), 128)],
                    home[j],
                ))
            yield
            for cp in cps:
                cp.wait_recv()
            mine = qbuf.at[k, xo(0), rows(zl * R, R)]
            cps = [send(mine, mine, at_zl(t)) for t in (1, 2, 3)]
            yield
            for cp in cps:
                cp.wait_recv()
            mine = qbuf.at[k, xo(0)]
            cr = send(mine, mine, at_x(1))
            cl = send(mine, mine, at_x(-1))
            yield
            cr.wait_recv()
            part = qbuf.at[k, xo(-1), 0 : 2 * R]
            rr = send(part, part, at_x(1))
            yield
            cl.wait_recv()
            part = qbuf.at[k, xo(1), 2 * R : 4 * R]
            rel = send(part, part, at_x(-1))
            yield
            rr.wait_recv()
            rel.wait_recv()
            for fh in range(2):
                whole = qbuf[k, 2 * fh : 2 * fh + 2].reshape(8 * R, 256)
                for i, part in enumerate(split3(whole)):
                    qs[self.pr, i, fh, self.pq : self.pq + 8 * R, :] = part
            yield

            def scores(i, carry):
                rw = pl.ds(pl.multiple_of(i * 128, 128), 128)
                qw = pl.ds(pl.multiple_of(self.pq + i * 128, 128), 128)
                acc = None
                for a, b in ((2, 0), (1, 1), (0, 2), (1, 0), (0, 1), (0, 0)):
                    for fh in range(2):
                        t = dot_nt(qs[self.pr, a, fh, qw, :], ds_[b, fh])
                        acc = t if acc is None else acc + t
                sbuf[k, rw, :] = acc
                return carry

            lax.fori_loop(0, 8 * R // 128, scores, 0)
            f = self.far
            self.m1 = send(sbuf.at[k, blk(4 * f)], rl.at[k, 0], at_y(2 * f))
            self.m2 = send(sbuf.at[k, blk(3 * f)], rl.at[k, 1], at_y(f))
            self.n1 = send(sbuf.at[k, blk(-3 * f)], rs.at[k, 0], at_y(-f))
            self.m4 = send(sbuf.at[k, blk(f)], rl.at[k, 3], at_y(f))
            self.n3 = send(sbuf.at[k, blk(-f)], rs.at[k, 2], at_y(-f))

        def reduce_far(self):
            k, f = self.k, self.far
            yield
            self.m1.wait_recv()
            self.m2.wait_recv()
            rl[k, 0] = rl[k, 0] + rl[k, 1] + sbuf[k, blk(2 * f), :]
            self.m3 = send(rl.at[k, 0], rl.at[k, 2], at_y(2 * f))

        def reduce_near(self):
            k, f = self.k, self.far
            yield
            self.n1.wait_recv()
            rs[k, 0] = rs[k, 0] + sbuf[k, blk(-2 * f), :]
            self.n2 = send(rs.at[k, 0], rs.at[k, 1], at_y(-2 * f))

        def join(self):
            k, f = self.k, self.far
            yield
            for cp in (self.m3, self.m4, self.n2, self.n3):
                cp.wait_recv()
            full = (sbuf[k, blk(0), :] + rs[k, 1] + rs[k, 2] + rl[k, 2] + rl[k, 3]) * INV
            sg[k, blk(0), :] = full
            mine = sg.at[k, blk(0)]
            self.a2 = send(mine, mine, at_y(2 * f))
            self.b2 = send(mine, mine, at_y(-2 * f))
            self.a1 = send(mine, mine, at_y(f))
            self.b1 = send(mine, mine, at_y(-f))
            tc = tcol[rows(64 * core + R * k, R), 0:1]
            top = jnp.max(full, axis=1, keepdims=True)
            total = jnp.sum(jnp.exp(full - top), axis=1, keepdims=True)
            hit = jnp.sum(jnp.where(tc == pidx, full, 0.0), axis=1, keepdims=True)
            ln = lax.broadcasted_iota(jnp.int32, (R, 128), 1)
            pack[k, 0:R, :] = jnp.where(ln == 0, top, jnp.where(ln == 1, total, jnp.where(ln == 2, hit, tc)))
            stx[k, zl * 4 + x] = pack[k].T[0:8]
            mine = stx.at[k, zl * 4 + x]
            cps = [send(mine, mine, at_grid(t)) for t in range(1, 16)]
            yield
            for cp in cps:
                cp.wait_recv()
            top, total, hit, tgt = merge(stx[k])
            mine = tg.at[k, blk_b(0)]
            tg[k, blk_b(0)] = tile(top + jnp.log(total), hit, tgt, tgt)
            self.g = [send(mine, mine, at_y(t)) for t in range(1, 8)]

        def gather_far(self):
            f = self.far
            yield
            self.a2.wait_recv()
            part = sg.at[self.k, blk(-2 * f)]
            self.a4 = send(part, part, at_y(2 * f))
            self.a3 = send(part, part, at_y(f))

        def gather_near(self):
            f = self.far
            yield
            self.b2.wait_recv()
            part = sg.at[self.k, blk(2 * f)]
            self.b3 = send(part, part, at_y(-f))

        def weights(self):
            k, pr, pq = self.k, self.pr, self.pq
            yield
            for cp in [self.a1, self.a3, self.a4, self.b1, self.b3] + self.g:
                cp.wait_recv()
            for b in range(8):
                tpack[k, b : b + 1, :] = tg[k, b, 0:1, :]
                tpack[k, 8 + b : 9 + b, :] = tg[k, b, 2:3, :]
            tt = tpack[k].T
            top = jnp.concatenate([tt[0:R, b : b + 1] for b in range(8)], axis=0)
            tgt = jnp.concatenate([tt[0:R, 8 + b : 9 + b] for b in range(8)], axis=0)
            w = (jnp.exp(sg[k] - top) - jnp.where(tgt == pidx, 1.0, 0.0)) * INV
            for i, part in enumerate(split2(w)):
                ws[pr, i, pq : pq + 8 * R, :] = part
            for i, part in enumerate(split2(w.T)):
                wts[pr, i, :, pq : pq + 8 * R] = part
            if k == K - 1:
                yield
                self.dd_pair(1 - zh)
                state["e0"] = send(dd.at[1 - zh, oth_p], ddr.at[0], other)

            rw = slice(pq, pq + 8 * R)
            for fh in range(2):
                acc = dot_nn(ws[pr, 1, rw, :], ds_[0, fh]) + dot_nn(ws[pr, 0, rw, :], ds_[1, fh])
                acc = acc + dot_nn(ws[pr, 0, rw, :], ds_[0, fh])
                dqp[k, 2 * fh] = acc[0 : 4 * R]
                dqp[k, 2 * fh + 1] = acc[4 * R : 8 * R]
            self.ca = send(dqp.at[k, xo(2), 0 : 2 * R], dqa.at[k], at_x(1))
            self.cb = send(dqp.at[k, xo(2), 2 * R : 4 * R], dqb.at[k], at_x(-1))
            self.c1 = send(dqp.at[k, xo(1), 2 * R : 4 * R], dxl.at[k, 2 * R : 4 * R], at_x(1))
            self.c2 = send(dqp.at[k, xo(-1), 0 : 2 * R], dxr.at[k, 0 : 2 * R], at_x(-1))

        def dd_pair(self, fh):
            pr = self.pr
            acc = dot_nn(wts[pr, 1], qs[pr, 0, fh])
            acc = acc + dot_nn(wts[pr, 0], qs[pr, 1, fh])
            acc = acc + dot_nn(wts[pr, 0], qs[pr, 0, fh])
            if pr == 0:
                dd[fh] = acc
            else:
                dd[fh] = dd[fh] + acc

        def documents_term(self):
            yield
            if self.k == K - 1:
                self.dd_pair(zh)
                state["e1"] = send(dd.at[zh, oth_p], ddr.at[1], other)
            elif self.k % 2 == 1:
                self.dd_pair(0)
                self.dd_pair(1)

        def sum_right(self):
            k = self.k
            yield
            self.ca.wait_recv()
            dqa[k] = dqa[k] + dqp[k, xo(1), 0 : 2 * R, :]
            self.c3 = send(dqa.at[k], dxl.at[k, 0 : 2 * R], at_x(1))

        def sum_left(self):
            k = self.k
            yield
            self.cb.wait_recv()
            dqb[k] = dqb[k] + dqp[k, xo(-1), 2 * R : 4 * R, :]
            self.c4 = send(dqb.at[k], dxr.at[k, 2 * R : 4 * R], at_x(-1))

        def sum_join(self):
            k = self.k
            yield
            for cp in (self.c1, self.c2, self.c3, self.c4):
                cp.wait_recv()
            dqt[k] = dqp[k, xo(0)] + dxl[k] + dxr[k]
            cps = [send(dqt.at[k, rows(lax.rem(zl + t, 4) * R, R)], dz.at[k, t - 1], at_zl(t)) for t in (1, 2, 3)]
            yield
            for cp in cps:
                cp.wait_recv()
            mine = rows(zl * R, R)
            dqt[k, mine, :] = dqt[k, mine, :] + dz[k, 0] + dz[k, 1] + dz[k, 2]
            cps = []
            for j in range(2):
                kc = core if j == 0 else 1 - core
                cps.append(send(
                    dqt.at[k, mine, pl.ds(pl.multiple_of(kc * 128, 128), 128)],
                    dqo.at[rows(64 * core + R * k, R)],
                    home[j],
                ))
            yield
            for cp in cps:
                cp.wait_recv()

    sub = lax.broadcasted_iota(jnp.int32, (8, 128), 0)

    def merge(st):
        m = st[:, 0, :]
        top = jnp.max(m, axis=0, keepdims=True)
        total = jnp.sum(st[:, 1, :] * jnp.exp(m - top), axis=0, keepdims=True)
        hit = jnp.sum(st[:, 2, :], axis=0, keepdims=True)
        return top, total, hit, st[0, 3:4, :]

    def tile(a, b, c, d):
        return jnp.where(sub == 0, a, jnp.where(sub == 1, b, jnp.where(sub == 2, c, d)))

    def ending():
        yield
        state["e0"].wait_recv()
        ddt[...] = dd[1 - zh, own_p, :] + ddr[0]
        last = yield from z_exchange(ddt, era, erb, ddz, ddz, 0)
        yield
        state["e1"].wait_recv()
        for cp in last:
            cp.wait_recv()
        dd_ref[...] = dd[zh, own_p, :] + ddr[1] + ddz[...]

    def loss():
        yield
        part = jnp.zeros((8, 128), F32)
        for k in range(K):
            part = part + jnp.where(lane < R, tg[k, :, 0, :] - tg[k, :, 1, :], 0.0)
        lsum[0] = jnp.broadcast_to(jnp.sum(part, keepdims=True), (8, 128))
        cp = send(lsum.at[0], lrecv.at[0], other)
        yield
        cp.wait_recv()
        lsum[1] = lsum[0] + lrecv[0]
        cp = send(lsum.at[1], lrecv.at[1], at_z(4))
        yield
        cp.wait_recv()
        loss_ref[0, 0] = jnp.sum((lsum[1] + lrecv[1])[0:1, 0:1]) * (1.0 / NQ)

    threads = [documents(), ending(), loss()]
    for k in range(K):
        c = Chunk(k)
        threads += [
            c.queries(), c.reduce_far(), c.reduce_near(), c.join(), c.gather_far(), c.gather_near(),
            c.weights(), c.documents_term(), c.sum_right(), c.sum_left(), c.sum_join(),
        ]
    ended = 0
    for t in ORDER:
        if next(threads[t], True):
            ended += 1
    assert ended == len(threads)
    dq_ref[...] = dqo[...]
    for cp in sends:
        cp.wait_send()


def fused(question_vectors, document_vectors, positive):
    vmem = pl.BlockSpec(memory_space=pltpu.VMEM)
    hbm = pl.BlockSpec(memory_space=pltpu.HBM)
    smem = pl.BlockSpec(memory_space=pltpu.SMEM)
    v = pltpu.VMEM
    loss, dq, dd = pl.pallas_call(
        kernel,
        out_shape=(
            jax.ShapeDtypeStruct((1, 1), F32),
            jax.ShapeDtypeStruct((128, 128), F32),
            jax.ShapeDtypeStruct((256, 256), F32),
        ),
        in_specs=[hbm, hbm, hbm],
        out_specs=(smem, vmem, vmem),
        scratch_shapes=[
            v((K, 4, 4 * R, 256), F32),
            v((K // 2, 3, 2, 16 * R, 256), BF16),
            v((2, 512, 256), F32),
            v((3, 2, 512, 256), BF16),
            v((128, 256), F32),
            v((128, 256), F32),
            v((K, 8 * R, 512), F32),
            v((K, 4, R, 512), F32),
            v((K, 3, R, 512), F32),
            v((K, 8 * R, 512), F32),
            v((K // 2, 2, 16 * R, 512), BF16),
            v((K // 2, 2, 512, 16 * R), BF16),
            v((128, 128), F32),
            v((K, 128, 128), F32),
            v((K, 128, 128), F32),
            v((K, 16, 8, 128), F32),
            v((K, 8, 8, 128), F32),
            v((K, 4, 4 * R, 256), F32),
            v((K, 2 * R, 256), F32),
            v((K, 2 * R, 256), F32),
            v((K, 4 * R, 256), F32),
            v((K, 4 * R, 256), F32),
            v((K, 3, R, 256), F32),
            v((K, 4 * R, 256), F32),
            v((128, 128), F32),
            v((2, 512, 256), F32),
            v((2, 256, 256), F32),
            v((256, 256), F32),
            v((128, 256), F32),
            v((128, 256), F32),
            v((256, 256), F32),
            v((2, 8, 128), F32),
            v((2, 8, 128), F32),
            v((1, 128), jnp.int32),
            pltpu.SemaphoreType.DMA((N_SEM,)),
            pltpu.SemaphoreType.DMA((N_SEM,)),
            pltpu.SemaphoreType.DMA((2,)),
        ],
        compiler_params=pltpu.CompilerParams(
            collective_id=0, has_side_effects=True, vmem_limit_bytes=40 * 1024 * 1024
        ),
        name="infonce",
    )(question_vectors, document_vectors, positive.reshape(1, 128))
    return loss.reshape(()), dq, dd


def solution(mesh):
    in_specs = (P("row", "col"), P("col", "row"), P("row"))
    out_specs = (P(), P("row", "col"), P("col", "row"))
    return jax.shard_map(fused, mesh=mesh, in_specs=in_specs, out_specs=out_specs, check_vma=False)
```
